256 devices in a mesh: tm: 8 (over y, x_lo), space: 32 (over z, x_hi, core).
Axes of the slice: x: 4 (x_hi: 2, x_lo: 2; x = x_hi * 2 + x_lo), y: 4, z: 8, core: 2. Of those that a mesh axis runs over, the one named last changes fastest.
Arguments:
- displace_at_opening: float32 [3, 256, 1024], P(None, 'space'), may hold values from -6 to 6
- resist_at_opening: float32 [256, 1024], P('space'), may hold values from 1 to 2
- operator_main_entries: float32 [256, 1024], P('space'), may hold values from 1 to 3
- thermal_forcing: float32 [3, 256, 1024], P(None, 'space'), may hold values from -6 to 6
- downward_link_matrix: float32 [3, 3, 256, 1024], P(None, None, 'space'), may hold values from 0.1 to 1
- lateral_link_matrix: float32 [3, 3, 256, 1024], P(None, None, 'space'), may hold values from 0.1 to 1
- heat_reading_array: float32 [64], replicated, may hold values from 0.5 to 1.5
- reading_lookup_per_tick: int32 [16], P('tm'), may hold values from 0 to 63
Outputs:
- u_end: float32 [8, 3, 256, 1024], P('tm', None, 'space')
- s_end: float32 [8, 256, 1024], P('tm', 'space')
The draws below stay inside these ranges and needn't reach their ends.
All inputs are finite; a program needn't handle non-finite values.
Results may differ from the reference program's by a relative error of at most 0.00018.
Values sent between devices are 32-bit elements; how exact they have to be, the bound alone decides.
A program may use at most 64 MiB of HBM per device.

```python
import jax
import jax.numpy as jnp
from jax import lax

W = 1024
MICRO_TICKS = 2
POLY_ROUNDS = 8
ANAND = 4
PASSES = 2
HISTORY_READINGS = 64
ROWS = 256
TOTAL_TICKS = 16
N_TM = 8


def edge_blocks(key, diag_low, off_low, off_high):
    key_diag, key_off = jax.random.split(key)
    diag_part = jax.random.uniform(key_diag, (3, 3, ROWS, W), jnp.float32, diag_low, 1.0)
    off_part = jax.random.uniform(key_off, (3, 3, ROWS, W), jnp.float32, off_low, off_high)
    identity = jnp.eye(3, dtype=jnp.float32)[:, :, None, None]
    return identity * diag_part + (1.0 - identity) * off_part


def draw_downward_link_matrix(key, part):
    key = jax.random.fold_in(key, 11)
    return edge_blocks(key, 0.5, 0.1, 0.3)


def draw_lateral_link_matrix(key, part):
    key = jax.random.fold_in(key, 23)
    return edge_blocks(key, 0.5, 0.1, 0.3)


def draw_operator_main_entries(key, part):
    key = jax.random.fold_in(key, 31)
    key_rough = jax.random.fold_in(key, 0)
    rough = jax.random.uniform(key_rough, (ROWS, W), jnp.float32, 0.0, 1.0)
    return 1.0 + 2.0 * rough


def draw_displace_at_opening(key, part):
    key = jax.random.fold_in(key, 41)
    key_rough = jax.random.fold_in(key, 0)
    return jnp.clip(jax.random.normal(key_rough, (3, ROWS, W), jnp.float32), -6.0, 6.0)


def draw_thermal_forcing(key, part):
    key = jax.random.fold_in(key, 53)
    key_rough = jax.random.fold_in(key, 0)
    return jnp.clip(jax.random.normal(key_rough, (3, ROWS, W), jnp.float32), -6.0, 6.0)


def touch_ends(entries, stream_key, low, largest):
    longest = entries.shape.index(max(entries.shape))
    spots = []
    for shift in (0, 1):
        where = [jax.random.randint(jax.random.fold_in(stream_key, axis), (), 0, length) for axis, length in enumerate(entries.shape)]
        where[longest] = (where[longest] + shift) % entries.shape[longest]
        spots.append(tuple(where))
    return entries.at[spots[0]].set(low).at[spots[1]].set(largest)


def block_scale(rng, extent, pieces, smallest, high):
    factor_of, own = 1.0, jax.random.fold_in(rng, 6)
    for dim, shards_of in pieces:
        steps = jnp.exp(jax.random.uniform(jax.random.fold_in(own, dim), (shards_of,), jnp.float32, smallest / len(pieces), high / len(pieces)))
        factor_of = factor_of * jnp.repeat(steps, extent[dim] // shards_of).reshape([-1 if axis == dim else 1 for axis in range(len(extent))])
    return factor_of


def setup_inputs(seed: int = 0) -> dict:
    keys = jax.random.split(jax.random.key(seed), 9)
    displace_at_opening = draw_displace_at_opening(jax.random.fold_in(keys[8], 71), 0)
    resist_at_opening = jnp.clip(1.0 + 1.0 * jax.random.uniform(keys[1], (ROWS, W), jnp.float32) ** block_scale(keys[1], (ROWS, W), ((0, 32),), -0.2, 0.2), 1.0, 2.0)
    operator_main_entries = draw_operator_main_entries(jax.random.fold_in(keys[8], 71), 0)
    thermal_forcing = draw_thermal_forcing(jax.random.fold_in(keys[8], 71), 0)
    downward_link_matrix = draw_downward_link_matrix(jax.random.fold_in(keys[8], 71), 0)
    lateral_link_matrix = draw_lateral_link_matrix(jax.random.fold_in(keys[8], 71), 0)
    heat_reading_array = jnp.clip(jax.random.uniform(keys[6], (HISTORY_READINGS,), jnp.float32, 0.5, 1.5), 0.5, 1.5)
    reading_lookup_per_tick = touch_ends(jax.random.randint(keys[7], (TOTAL_TICKS,), 0, HISTORY_READINGS), jax.random.fold_in(keys[7], 1), 0, HISTORY_READINGS - 1).astype(jnp.int32)
    return dict(displace_at_opening=displace_at_opening, resist_at_opening=resist_at_opening, operator_main_entries=operator_main_entries, thermal_forcing=thermal_forcing, downward_link_matrix=downward_link_matrix, lateral_link_matrix=lateral_link_matrix, heat_reading_array=heat_reading_array, reading_lookup_per_tick=reading_lookup_per_tick)


coupling = 0.9 / 6.4
mass_portion = 0.3
hardening = 0.25
saturation = 3.0
march_single_tick = 0.5
half_width = 0.9

def make_blocks(downward_link_matrix, lateral_link_matrix, operator_main_entries, north_edge, north_diag, south_diag):
    west_edge = jnp.pad(lateral_link_matrix, ((0, 0), (0, 0), (0, 0), (1, 0)))[..., :-1]
    west_diag = jnp.pad(operator_main_entries, ((0, 0), (1, 0)))[:, :-1]
    east_diag = jnp.pad(operator_main_entries, ((0, 0), (0, 1)))[:, 1:]
    north_block = coupling * jnp.minimum(operator_main_entries, north_diag) * jnp.transpose(north_edge, (1, 0, 2, 3))
    south_block = coupling * jnp.minimum(operator_main_entries, south_diag) * downward_link_matrix
    west_block = coupling * jnp.minimum(operator_main_entries, west_diag) * jnp.transpose(west_edge, (1, 0, 2, 3))
    east_block = coupling * jnp.minimum(operator_main_entries, east_diag) * lateral_link_matrix
    return (north_block, south_block, west_block, east_block)

def couple(blocks, values_field, padded):
    north_block, south_block, west_block, east_block = blocks
    from_west = jnp.pad(values_field, ((0, 0), (0, 0), (1, 0)))[..., :-1]
    from_east = jnp.pad(values_field, ((0, 0), (0, 0), (0, 1)))[..., 1:]
    summed = lax.optimization_barrier(jnp.sum(north_block * padded[None, :, :-2], axis=1))
    summed = summed + lax.optimization_barrier(jnp.sum(south_block * padded[None, :, 2:], axis=1))
    summed = summed + lax.optimization_barrier(jnp.sum(west_block * from_west[None], axis=1))
    summed = summed + lax.optimization_barrier(jnp.sum(east_block * from_east[None], axis=1))
    return summed

def implicit_march_rule(present_unknowns, present_heat_level, tick_duration, round_total, invoke_mapping, operator_main_entries, thermal_forcing):
    prescribed_elongation = present_unknowns[:3]
    activation_multiplier = jnp.exp(2.0 - 2.0 / present_heat_level)
    tangential_traction = jnp.sqrt(lax.optimization_barrier(jnp.mean(prescribed_elongation * prescribed_elongation, axis=0)) + 1.0)
    resist_old = jnp.exp(present_unknowns[3])
    resist = resist_old
    for anand_index in range(ANAND):
        creep_speed = activation_multiplier * jnp.tanh(tangential_traction / resist)
        resist = resist_old + tick_duration * hardening * creep_speed * (1.0 - resist / saturation)
    creep_speed = activation_multiplier * jnp.tanh(tangential_traction / resist)
    target_level = mass_portion * operator_main_entries * prescribed_elongation + tick_duration * (present_heat_level * thermal_forcing - creep_speed * prescribed_elongation / tangential_traction)
    iterate = prescribed_elongation
    residual_part = target_level - invoke_mapping(iterate)
    direction = residual_part / operator_main_entries
    cheb_weight = half_width
    for sweep_index in range(round_total):
        iterate = iterate + direction
        if sweep_index < round_total - 1:
            residual_part = residual_part - invoke_mapping(direction)
            weight_next = 1.0 / (2.0 / half_width - cheb_weight)
            direction = weight_next * cheb_weight * direction + 2.0 * weight_next / half_width * residual_part / operator_main_entries
            cheb_weight = weight_next
    return jnp.concatenate([iterate, jnp.log(resist)[None]], axis=0)

def reference(displace_at_opening, resist_at_opening, operator_main_entries, thermal_forcing, downward_link_matrix, lateral_link_matrix, heat_reading_array, reading_lookup_per_tick):
    north_edge = jnp.pad(downward_link_matrix, ((0, 0), (0, 0), (1, 0), (0, 0)))[:, :, :-1]
    north_diag = jnp.pad(operator_main_entries, ((1, 0), (0, 0)))[:-1]
    south_diag = jnp.pad(operator_main_entries, ((0, 1), (0, 0)))[1:]
    blocks = make_blocks(downward_link_matrix, lateral_link_matrix, operator_main_entries, north_edge, north_diag, south_diag)

    def invoke_mapping(values_field):
        padded = jnp.pad(values_field, ((0, 0), (1, 1), (0, 0)))
        return operator_main_entries * values_field + couple(blocks, values_field, padded)
    heat_trace = heat_reading_array[reading_lookup_per_tick].reshape(N_TM, MICRO_TICKS)

    def cheap_predictor(present_unknowns, horizon_location):
        return implicit_march_rule(present_unknowns, jnp.mean(heat_trace[horizon_location]), MICRO_TICKS * march_single_tick, 1, invoke_mapping, operator_main_entries, thermal_forcing)

    def fine(present_unknowns, horizon_location):
        for tick_location in range(MICRO_TICKS):
            present_unknowns = implicit_march_rule(present_unknowns, heat_trace[horizon_location, tick_location], march_single_tick, POLY_ROUNDS, invoke_mapping, operator_main_entries, thermal_forcing)
        return present_unknowns
    state_zero = jnp.concatenate([displace_at_opening, jnp.log(resist_at_opening)[None]], axis=0)
    starts = []
    coarse_ends = []
    slice_ends = []
    slice_start = state_zero
    for horizon_location in range(N_TM):
        starts.append(slice_start)
        coarse_end = cheap_predictor(slice_start, horizon_location)
        coarse_ends.append(coarse_end)
        slice_ends.append(coarse_end)
        slice_start = coarse_end
    for pass_index in range(PASSES):
        corrections = [fine(starts[horizon_location], horizon_location) - coarse_ends[horizon_location] for horizon_location in range(N_TM)]
        starts = []
        coarse_ends = []
        slice_ends = []
        slice_start = state_zero
        for horizon_location in range(N_TM):
            starts.append(slice_start)
            coarse_end = cheap_predictor(slice_start, horizon_location)
            coarse_ends.append(coarse_end)
            slice_end = coarse_end + corrections[horizon_location]
            slice_ends.append(slice_end)
            slice_start = slice_end
    final_states = jnp.stack(slice_ends)
    return (final_states[:, :3], jnp.exp(final_states[:, 3]))
```

```python
import functools

import jax
import jax.numpy as jnp
from jax import lax
from jax.experimental import pallas as pl
from jax.experimental.pallas import tpu as pltpu
from jax.sharding import PartitionSpec as P

COUPLING = 0.9 / 6.4
MASS = 0.3
HARDENING = 0.25
SATURATION = 3.0
TICK = 0.5
HALF_WIDTH = 0.9
SWEEPS = 8
ANAND = 4
ROWS = 24
OWN = 8
PLANES = 26
S0, L0, D0, F0, U0 = 0, 9, 18, 19, 22
MESH = pl.DeviceIdType.MESH


def chebyshev_weights():
    weights, w = [], HALF_WIDTH
    for _ in range(SWEEPS - 1):
        nxt = 1.0 / (2.0 / HALF_WIDTH - w)
        weights.append((nxt * w, 2.0 * nxt / HALF_WIDTH))
        w = nxt
    return weights


def at(row):
    if isinstance(row, int):
        return pl.ds(8 * row, 8)
    return pl.ds(pl.multiple_of(8 * row, 8), 8)


def span(row, count):
    if isinstance(row, int):
        return pl.ds(8 * row, 8 * count)
    return pl.ds(pl.multiple_of(8 * row, 8), 8 * count)


def kernel(
    n_tm, n_sp,
    u_in, s_in, d_in, f_in, down_in, lat_in, heat, look,
    u_out, s_out,
    raw, U, Pd, Z, E, GU, C, VOUT, VIN, CIN, XH, TH, ssem, rsem,
):
    n = lax.axis_index("tm")
    sp = lax.axis_index("space")
    up, dn = lax.rem(sp + n_sp - 1, n_sp), lax.rem(sp + 1, n_sp)
    lane = lax.broadcasted_iota(jnp.int32, (8, 128), 1)
    sub = lax.broadcasted_iota(jnp.int32, (8, 128), 0)
    first_lane, last_lane = lane == 0, lane == 127

    barrier = pltpu.get_barrier_semaphore()
    peers = [(lax.rem(n + d, n_tm), sp) for d in range(1, n_tm)]
    for d in (0, 1, 2, n_tm - 2, n_tm - 1):
        for side in (up, dn):
            peers.append((lax.rem(n + d, n_tm), side))
    for peer in peers:
        pl.semaphore_signal(barrier, inc=1, device_id=peer, device_id_type=MESH)

    def copy(src, dst, sem, who):
        return pltpu.make_async_remote_copy(
            src_ref=src, dst_ref=dst, send_sem=ssem.at[sem], recv_sem=rsem.at[sem],
            device_id=who, device_id_type=MESH,
        )

    def pack(plane, tile_of):
        for c in range(8):
            raw[plane, pl.ds(8 * OWN + c, 8, stride=8), :] = tile_of(pl.ds(128 * c, 128))

    for a in range(3):
        for b in range(3):
            pack(S0 + 3 * a + b, lambda cols, a=a, b=b: down_in[a, b, :, cols])
            pack(L0 + 3 * a + b, lambda cols, a=a, b=b: lat_in[a, b, :, cols])
        pack(F0 + a, lambda cols, a=a: f_in[a, :, cols])
        pack(U0 + a, lambda cols, a=a: u_in[a, :, cols])
    pack(D0, lambda cols: d_in[:, cols])
    pack(U0 + 3, lambda cols: s_in[:, cols])
    for k in range(2):
        TH[n, pl.ds(8 * k, 8), :] = jnp.full((8, 128), heat[look[k]], jnp.float32)

    pl.semaphore_wait(barrier, len(peers))

    own_raw = raw.at[:, span(OWN, 8), :]
    halos = [
        copy(own_raw, raw.at[:, span(0, 8), :], 0, (n, dn)),
        copy(own_raw, raw.at[:, span(16, 8), :], 1, (n, up)),
    ]
    heats = [
        copy(TH.at[n], TH.at[n], 1 + d, (lax.rem(n + d, n_tm), sp)) for d in range(1, n_tm)
    ]
    for c in halos + heats:
        c.start()
    for d in range(1, n_tm):
        src = lax.rem(n + n_tm - d, n_tm)
        copy(TH.at[src], TH.at[src], 1 + d, (src, sp)).wait_recv()
    for c in halos:
        c.wait()
    for c in heats:
        c.wait_send()

    def east(v):
        a = pltpu.roll(v, 127, 1)
        return jnp.where(last_lane, pltpu.roll(a, 7, 0), a)

    def west(v):
        a = pltpu.roll(v, 1, 1)
        return jnp.where(first_lane, pltpu.roll(a, 1, 0), a)

    corner = (lane == 127) & (sub == 7)

    def build(r, diag):
        below = raw[D0, at(jnp.minimum(r + 1, ROWS - 1)), :]
        seam = ((sp == 0) & (r == OWN - 1)) | ((sp == n_sp - 1) & (r == 2 * OWN - 1))
        cs = COUPLING * jnp.minimum(diag, below) * jnp.where(seam, 0.0, 1.0)
        cl = jnp.where(corner, 0.0, COUPLING * jnp.minimum(diag, east(diag)))
        for k in range(9):
            raw[S0 + k, at(r), :] = raw[S0 + k, at(r), :] * cs
            raw[L0 + k, at(r), :] = raw[L0 + k, at(r), :] * cl
        for k in range(4):
            U[k, at(r), :] = raw[U0 + k, at(r), :]
        raw[D0, at(r), :] = 1.0 / diag
        return below

    lax.fori_loop(0, ROWS, build, raw[D0, at(0), :])

    def heat_of(slice_index, tick):
        return TH[slice_index, pl.ds(8 * tick, 1), :]

    def mean_heat(slice_index):
        return 0.5 * (TH[slice_index, 0:1, :] + TH[slice_index, 8:9, :])

    def creep(load, store_s, t, h, lo, count, chunk):
        rate = jnp.exp(2.0 - 2.0 / t)

        def body(i, _):
            r = lo + i * chunk
            u0, u1, u2, s = (load(k, r, chunk) for k in range(4))
            q2 = (u0 * u0 + u1 * u1 + u2 * u2) * (1.0 / 3.0) + 1.0
            qi = lax.rsqrt(q2)
            q = q2 * qi
            x = s
            for _ in range(ANAND):
                x = s + (h * HARDENING) * rate * jnp.tanh(q / x) * (1.0 - x * (1.0 / SATURATION))
            E[span(r, chunk), :] = (h * rate) * jnp.tanh(q / x) * qi
            store_s(r, chunk, x)
            return 0

        lax.fori_loop(0, count // chunk, body, 0)

    def stencil(load, lo, hi, emit):
        p = [load(b, lo - 1) for b in range(3)]
        s = [[raw[S0 + 3 * a + b, at(lo - 1), :] for b in range(3)] for a in range(3)]
        north = [s[0][b] * p[0] + s[1][b] * p[1] + s[2][b] * p[2] for b in range(3)]
        p = [load(b, lo) for b in range(3)]
        for r in range(lo, hi):
            nxt = [load(b, r + 1) for b in range(3)]
            s = [[raw[S0 + 3 * a + b, at(r), :] for b in range(3)] for a in range(3)]
            l = [[raw[L0 + 3 * a + b, at(r), :] for b in range(3)] for a in range(3)]
            pe = [east(p[b]) for b in range(3)]
            wf = [west(l[0][b] * p[0] + l[1][b] * p[1] + l[2][b] * p[2]) for b in range(3)]
            cv = []
            for a in range(3):
                south = s[a][0] * nxt[0] + s[a][1] * nxt[1] + s[a][2] * nxt[2]
                right = l[a][0] * pe[0] + l[a][1] * pe[1] + l[a][2] * pe[2]
                cv.append((north[a] + wf[a]) + (south + right))
            north = [s[0][b] * p[0] + s[1][b] * p[1] + s[2][b] * p[2] for b in range(3)]
            emit(r, p, cv)
            p = nxt

    def force(r, v, cv, th):
        inv, e = raw[D0, at(r), :], E[at(r), :]
        return [
            inv * (th * raw[F0 + a, at(r), :] - e * v[a] - cv[a]) for a in range(3)
        ]

    def fine_tick(t):
        h = TICK

        def load(k, r, c):
            return U[k, span(r, c), :]

        def store_s(r, c, x):
            U[3, span(r, c), :] = x

        creep(load, store_s, t, h, 0, ROWS, 8)
        th = h * t

        def first(r, v, cv):
            g = force(r, v, cv, th)
            for a in range(3):
                z = g[a] - (1.0 - MASS) * v[a]
                Z[a, at(r), :] = z
                Pd[a, at(r), :] = z
                if OWN <= r < 2 * OWN:
                    U[a, at(r), :] = v[a] + z

        stencil(lambda b, r: U[b, at(r), :], 1, ROWS - 1, first)
        for k, (alpha, beta) in enumerate(chebyshev_weights()):
            def sweep(r, v, cv, alpha=alpha, beta=beta, k=k):
                inv = raw[D0, at(r), :]
                for a in range(3):
                    z = Z[a, at(r), :] - v[a] - inv * cv[a]
                    p = alpha * v[a] + beta * z
                    if k < SWEEPS - 2:
                        Z[a, at(r), :] = z
                        Pd[a, at(r), :] = p
                    if OWN <= r < 2 * OWN:
                        U[a, at(r), :] = U[a, at(r), :] + p

            stencil(lambda b, r: Pd[b, at(r), :], 2 + k, ROWS - 2 - k, sweep)

    def exchange(slot, sem, planes):
        own = U.at[pl.ds(0, planes), span(OWN, 8), :]
        pair = [
            copy(own, XH.at[slot, 0, pl.ds(0, planes)], sem, (n, dn)),
            copy(own, XH.at[slot, 1, pl.ds(0, planes)], sem + 1, (n, up)),
        ]
        for c in pair:
            c.start()
        for c in pair:
            c.wait()
        for k in range(planes):
            U[k, span(0, 8), :] = XH[slot, 0, k]
            U[k, span(16, 8), :] = XH[slot, 1, k]

    def coarse_own():
        t = mean_heat(n)

        def load(k, r, c):
            return U[k, span(r, c), :]

        def store_s(r, c, x):
            GU[3, span(r - OWN, c), :] = x

        creep(load, store_s, t, 2.0 * TICK, OWN, 8, 8)

        def emit(r, v, cv):
            g = force(r, v, cv, 2.0 * TICK * t)
            for a in range(3):
                GU[a, at(r - OWN), :] = MASS * v[a] + g[a]

        stencil(lambda b, r: U[b, at(r), :], OWN, 2 * OWN, emit)

    def coarse_step(m, _):
        t = mean_heat(m)

        def load(k, r, c):
            return U[k, span(r, c), :]

        def store_s(r, c, x):
            U[3, span(r, c), :] = x

        creep(load, store_s, t, 2.0 * TICK, 0, ROWS, 8)

        def emit(r, v, cv):
            g = force(r, v, cv, 2.0 * TICK * t)
            for a in range(3):
                U[a, at(r), :] = MASS * v[a] + g[a]

        stencil(lambda b, r: U[b, at(r), :], 1, ROWS - 1, emit)
        return 0

    lax.fori_loop(0, n, coarse_step, 0)

    @pl.when(n > 0)
    def _():
        coarse_own()
        exchange(0, 9, 4)

    odd = lax.rem(n, 2) == 1
    even = (lax.rem(n, 2) == 0) & (n > 0)

    def to_next(p):
        nxt = lax.rem(n + 1, n_tm)
        base = 17 + 6 * p
        return [
            copy(VOUT.at[p], VIN.at[p, :, span(OWN, 8), :], base, (nxt, sp)),
            copy(VOUT.at[p], VIN.at[p, :, span(16, 8), :], base + 1, (nxt, up)),
            copy(VOUT.at[p], VIN.at[p, :, span(0, 8), :], base + 2, (nxt, dn)),
        ]

    def to_second(p):
        nxt = lax.rem(n + 2, n_tm)
        base = 20 + 6 * p
        return [
            copy(VOUT.at[p], VIN.at[p, :, span(OWN, 8), :], base, (nxt, sp)),
            copy(VOUT.at[p, :, span(0, 2), :], VIN.at[p, :, span(16, 2), :], base + 1, (nxt, up)),
            copy(VOUT.at[p, :, span(6, 2), :], VIN.at[p, :, span(6, 2), :], base + 2, (nxt, dn)),
        ]

    def corrections(p):
        nxt = lax.rem(n + 1, n_tm)
        base = 29 + 3 * p
        return [
            copy(C.at[p], CIN.at[p, :, span(OWN, 8), :], base, (nxt, sp)),
            copy(C.at[p, :, span(0, 1), :], CIN.at[p, :, span(16, 1), :], base + 1, (nxt, up)),
            copy(C.at[p, :, span(7, 1), :], CIN.at[p, :, span(7, 1), :], base + 2, (nxt, dn)),
        ]

    def one_pass(p, _):
        @pl.when((n > 0) | (p == 0))
        def _():
            def tick(i, _):
                @pl.when(i == 1)
                def _():
                    exchange(1 + 2 * p, 11 + 4 * p, 3)

                fine_tick(heat_of(n, i))
                return 0

            lax.fori_loop(0, 2, tick, 0)

        @pl.when(n > 0)
        def _():
            for a in range(3):
                C[p, a] = U[a, span(OWN, 8), :] - GU[a]
            C[p, 3] = U[3, span(OWN, 8), :] / GU[3]

        @pl.when(odd & (n < n_tm - 1))
        def _():
            for c in corrections(p):
                c.start()

        @pl.when(odd)
        def _():
            for c in to_next(p):
                c.wait_recv()
            for k in range(4):
                for r in range(3):
                    U[k, span(8 * r, 8), :] = VIN[p, k, span(8 * r, 8), :]

        @pl.when(even)
        def _():
            for c in to_second(p):
                c.wait_recv()
            for c in corrections(p):
                c.wait_recv()
            t = mean_heat(n - 1)

            def load(k, r, c):
                return VIN[p, k, span(r, c), :]

            def store_s(r, c, x):
                U[3, span(r, c), :] = x * CIN[p, 3, span(r, c), :]

            creep(load, store_s, t, 2.0 * TICK, OWN - 1, 10, 10)

            def emit(r, v, cv):
                g = force(r, v, cv, 2.0 * TICK * t)
                for a in range(3):
                    U[a, at(r), :] = MASS * v[a] + g[a] + CIN[p, a, at(r), :]

            stencil(lambda b, r: VIN[p, b, at(r), :], OWN - 1, 2 * OWN + 1, emit)

        @pl.when(n == 0)
        def _():
            for k in range(4):
                VOUT[p, k] = U[k, span(OWN, 8), :]

        @pl.when(n > 0)
        def _():
            coarse_own()
            for a in range(3):
                VOUT[p, a] = GU[a] + C[p, a]
            VOUT[p, 3] = GU[3] * C[p, 3]

        @pl.when(jnp.logical_not(odd))
        def _():
            for c in to_next(p):
                c.start()

        @pl.when(jnp.logical_not(odd) & (n < n_tm - 2))
        def _():
            for c in to_second(p):
                c.start()

        @pl.when(even & (p == 0))
        def _():
            exchange(2, 13, 4)

        return 0

    lax.fori_loop(0, 2, one_pass, 0)

    for c in range(8):
        cols = pl.ds(128 * c, 128)
        for a in range(3):
            u_out[0, a, :, cols] = VOUT[1, a, pl.ds(c, 8, stride=8), :]
        s_out[0, :, cols] = VOUT[1, 3, pl.ds(c, 8, stride=8), :]

    for p in range(2):
        @pl.when(odd & (n < n_tm - 1))
        def _():
            for c in corrections(p):
                c.wait_send()

        @pl.when(jnp.logical_not(odd))
        def _():
            for c in to_next(p):
                c.wait_send()

        @pl.when(jnp.logical_not(odd) & (n < n_tm - 2))
        def _():
            for c in to_second(p):
                c.wait_send()


def per_device(n_tm, n_sp, u, s, d, f, down, lat, heat, look):
    vmem = pl.BlockSpec(memory_space=pltpu.VMEM)
    smem = pl.BlockSpec(memory_space=pltpu.SMEM)
    f32 = jnp.float32
    return pl.pallas_call(
        functools.partial(kernel, n_tm, n_sp),
        out_shape=(
            jax.ShapeDtypeStruct((1, 3, 8, 1024), f32),
            jax.ShapeDtypeStruct((1, 8, 1024), f32),
        ),
        in_specs=[vmem] * 6 + [smem] * 2,
        out_specs=(vmem, vmem),
        scratch_shapes=[
            pltpu.VMEM((PLANES, 8 * ROWS, 128), f32),
            pltpu.VMEM((4, 8 * ROWS, 128), f32),
            pltpu.VMEM((3, 8 * ROWS, 128), f32),
            pltpu.VMEM((3, 8 * ROWS, 128), f32),
            pltpu.VMEM((8 * ROWS, 128), f32),
            pltpu.VMEM((4, 64, 128), f32),
            pltpu.VMEM((2, 4, 64, 128), f32),
            pltpu.VMEM((2, 4, 64, 128), f32),
            pltpu.VMEM((2, 4, 8 * ROWS, 128), f32),
            pltpu.VMEM((2, 4, 8 * ROWS, 128), f32),
            pltpu.VMEM((4, 2, 4, 64, 128), f32),
            pltpu.VMEM((8, 16, 128), f32),
            pltpu.SemaphoreType.DMA((35,)),
            pltpu.SemaphoreType.DMA((35,)),
        ],
        compiler_params=pltpu.CompilerParams(
            collective_id=0, has_side_effects=True, vmem_limit_bytes=32 * 1024 * 1024
        ),
        name="parareal",
    )(u, s, d, f, down, lat, heat, look)


def solution(mesh):
    return jax.shard_map(
        functools.partial(per_device, mesh.shape["tm"], mesh.shape["space"]),
        mesh=mesh,
        in_specs=(
            P(None, "space", None),
            P("space", None),
            P("space", None),
            P(None, "space", None),
            P(None, None, "space", None),
            P(None, None, "space", None),
            P(),
            P("tm"),
        ),
        out_specs=(P("tm", None, "space", None), P("tm", "space", None)),
        check_vma=False,
    )
```

```python
import functools

import jax
import jax.numpy as jnp
from jax import lax
from jax.experimental import pallas as pl
from jax.experimental.pallas import tpu as pltpu
from jax.sharding import PartitionSpec as P

COUPLING = 0.9 / 6.4
MASS = 0.3
HARDENING = 0.25
SATURATION = 3.0
TICK = 0.5
HALF_WIDTH = 0.9
SWEEPS = 8
ANAND = 4
ROWS = 26
OWN = 9
ABOVE, BELOW = 1, 17
PLANES = 26
S0, D0, U0, F0, L0 = 0, 9, 10, 14, 17
MESH = pl.DeviceIdType.MESH


def chebyshev_weights():
    weights, w = [], HALF_WIDTH
    for _ in range(SWEEPS - 1):
        nxt = 1.0 / (2.0 / HALF_WIDTH - w)
        weights.append((nxt * w, 2.0 * nxt / HALF_WIDTH))
        w = nxt
    return weights


def at(row):
    if isinstance(row, int):
        return pl.ds(8 * row, 8)
    return pl.ds(pl.multiple_of(8 * row, 8), 8)


def span(row, count):
    if isinstance(row, int):
        return pl.ds(8 * row, 8 * count)
    return pl.ds(pl.multiple_of(8 * row, 8), 8 * count)


def kernel(
    n_tm, n_sp,
    u_hbm, s_hbm, d_hbm, f_hbm, down_hbm, lat_hbm, heat_hbm, look_hbm,
    u_out, s_out,
    u_in, s_in, d_in, f_in, down_in, lat_in, heat, look,
    raw, DI, U, Pd, Z, E, GU, C, VOUT, VIN, CIN, XH, TH, lsem, ssem, rsem,
):
    n = lax.axis_index("tm")
    sp = lax.axis_index("space")
    up, dn = lax.rem(sp + n_sp - 1, n_sp), lax.rem(sp + 1, n_sp)
    up2, dn2 = lax.rem(sp + n_sp - 2, n_sp), lax.rem(sp + 2, n_sp)
    lane = lax.broadcasted_iota(jnp.int32, (8, 128), 1)
    sub = lax.broadcasted_iota(jnp.int32, (8, 128), 0)
    first_lane, last_lane = lane == 0, lane == 127

    loads = [
        pltpu.make_async_copy(src, dst, lsem.at[k])
        for k, (src, dst) in enumerate(
            [(look_hbm, look), (heat_hbm, heat), (down_hbm, down_in), (lat_hbm, lat_in),
             (u_hbm, u_in), (s_hbm, s_in), (d_hbm, d_in), (f_hbm, f_in)]
        )
    ]
    for c in loads:
        c.start()

    barrier = pltpu.get_barrier_semaphore()
    peers = [(lax.rem(n + d, n_tm), sp) for d in range(1, n_tm)]
    for d in (0, 1, 2, n_tm - 2, n_tm - 1):
        for side in (up, dn):
            peers.append((lax.rem(n + d, n_tm), side))
    peers += [(n, up2), (n, dn2)]
    for peer in peers:
        pl.semaphore_signal(barrier, inc=1, device_id=peer, device_id_type=MESH)

    def copy(src, dst, sem, who):
        return pltpu.make_async_remote_copy(
            src_ref=src, dst_ref=dst, send_sem=ssem.at[sem], recv_sem=rsem.at[sem],
            device_id=who, device_id_type=MESH,
        )

    def pack(plane, tile_of):
        for c in range(8):
            raw[plane, pl.ds(8 * OWN + c, 8, stride=8), :] = tile_of(pl.ds(128 * c, 128))

    for c in loads:
        c.wait()
    for a in range(3):
        for b in range(3):
            pack(S0 + 3 * a + b, lambda cols, a=a, b=b: down_in[a, b, :, cols])
            pack(L0 + 3 * a + b, lambda cols, a=a, b=b: lat_in[a, b, :, cols])
        pack(F0 + a, lambda cols, a=a: f_in[a, :, cols])
        pack(U0 + a, lambda cols, a=a: u_in[a, :, cols])
    pack(D0, lambda cols: d_in[:, cols])
    pack(U0 + 3, lambda cols: s_in[:, cols])
    for k in range(2):
        TH[n, pl.ds(8 * k, 8), :] = jnp.full((8, 128), heat[look[k]], jnp.float32)

    pl.semaphore_wait(barrier, len(peers))

    core = lax.rem(sp, 2)
    y = n // 2
    sibling = sp + 1 - 2 * core
    outer = jnp.where(core == 0, up, dn)
    to_sibling = jnp.where(core == 0, ABOVE, BELOW)
    to_outer = jnp.where(core == 0, BELOW, ABOVE)
    from_outer = jnp.where(core == 0, ABOVE, BELOW)
    across = (n + 1 - 2 * lax.rem(n, 2), outer)
    shared = copy(raw.at[:, span(OWN + y, 1), :], raw.at[:, span(to_outer + y, 1), :], 1, across)
    shared.start()
    straight = [
        copy(raw.at[:, span(OWN + 4, 4), :], raw.at[:, span(to_outer + 4, 4), :], 2, across),
        copy(raw.at[:, span(OWN, 8), :], raw.at[:, span(to_sibling, 8), :], 0, (n, sibling)),
        copy(
            raw.at[pl.ds(0, F0 - 1), span(OWN + 7, 1), :],
            raw.at[pl.ds(0, F0 - 1), span(0, 1), :], 6, (n, dn2),
        ),
        copy(
            raw.at[pl.ds(D0, 4), span(OWN, 1), :],
            raw.at[pl.ds(D0, 4), span(ROWS - 1, 1), :], 7, (n, up2),
        ),
    ]
    heats = [
        copy(TH.at[n], TH.at[n], 7 + d, (lax.rem(n + d, n_tm), sp)) for d in range(1, n_tm)
    ]
    for c in straight + heats:
        c.start()
    shared.wait_recv()
    passed = raw.at[:, span(from_outer + y, 1), :]
    passing = [
        copy(passed, passed, 2 + d, (lax.rem(n + 2 * d, n_tm), sp)) for d in (1, 2, 3)
    ]
    for c in passing:
        c.start()
    for d in range(1, n_tm):
        src = lax.rem(n + n_tm - d, n_tm)
        copy(TH.at[src], TH.at[src], 7 + d, (src, sp)).wait_recv()
    for c in straight:
        c.wait()
    for d in (1, 2, 3):
        src = lax.rem(n + n_tm - 2 * d, n_tm)
        row = raw.at[:, span(from_outer + src // 2, 1), :]
        copy(row, row, 2 + d, (src, sp)).wait_recv()
    shared.wait_send()
    for c in heats + passing:
        c.wait_send()

    def east(v):
        a = pltpu.roll(v, 127, 1)
        return jnp.where(last_lane, pltpu.roll(a, 7, 0), a)

    def west(v):
        a = pltpu.roll(v, 1, 1)
        return jnp.where(first_lane, pltpu.roll(a, 1, 0), a)

    corner = (lane == 127) & (sub == 7)
    for r in range(ROWS):
        diag = raw[D0, at(r), :]
        if r < ROWS - 1:
            row = 8 * sp + (r - OWN)
            seam = (row == -1) | (row == 8 * n_sp - 1)
            below = raw[D0, at(r + 1), :]
            cs = COUPLING * jnp.minimum(diag, below) * jnp.where(seam, 0.0, 1.0)
            for k in range(9):
                raw[S0 + k, at(r), :] = raw[S0 + k, at(r), :] * cs
        if 0 < r < ROWS - 1:
            cl = jnp.where(corner, 0.0, COUPLING * jnp.minimum(diag, east(diag)))
            for k in range(9):
                raw[L0 + k, at(r), :] = raw[L0 + k, at(r), :] * cl
            DI[at(r), :] = 1.0 / diag
            U[3, at(r), :] = raw[U0 + 3, at(r), :]
        for k in range(3):
            U[k, at(r), :] = raw[U0 + k, at(r), :]

    def heat_of(slice_index, tick):
        return TH[slice_index, pl.ds(8 * tick, 1), :]

    def mean_heat(slice_index):
        return 0.5 * (TH[slice_index, 0:1, :] + TH[slice_index, 8:9, :])

    def creep(load, store_s, t, h, lo, count, chunk):
        rate = jnp.exp(2.0 - 2.0 / t)

        def body(i, _):
            r = lo + i * chunk
            u0, u1, u2, s = (load(k, r, chunk) for k in range(4))
            q2 = (u0 * u0 + u1 * u1 + u2 * u2) * (1.0 / 3.0) + 1.0
            qi = lax.rsqrt(q2)
            q = q2 * qi
            x = s
            for _ in range(ANAND):
                x = s + (h * HARDENING) * rate * jnp.tanh(q / x) * (1.0 - x * (1.0 / SATURATION))
            E[span(r, chunk), :] = (h * rate) * jnp.tanh(q / x) * qi
            store_s(r, chunk, x)
            return 0

        lax.fori_loop(0, count // chunk, body, 0)

    def stencil(load, lo, hi, emit):
        p = [load(b, lo - 1) for b in range(3)]
        s = [[raw[S0 + 3 * a + b, at(lo - 1), :] for b in range(3)] for a in range(3)]
        north = [s[0][b] * p[0] + s[1][b] * p[1] + s[2][b] * p[2] for b in range(3)]
        p = [load(b, lo) for b in range(3)]
        for r in range(lo, hi):
            nxt = [load(b, r + 1) for b in range(3)]
            s = [[raw[S0 + 3 * a + b, at(r), :] for b in range(3)] for a in range(3)]
            l = [[raw[L0 + 3 * a + b, at(r), :] for b in range(3)] for a in range(3)]
            pe = [east(p[b]) for b in range(3)]
            wf = [west(l[0][b] * p[0] + l[1][b] * p[1] + l[2][b] * p[2]) for b in range(3)]
            cv = []
            for a in range(3):
                south = s[a][0] * nxt[0] + s[a][1] * nxt[1] + s[a][2] * nxt[2]
                right = l[a][0] * pe[0] + l[a][1] * pe[1] + l[a][2] * pe[2]
                cv.append((north[a] + wf[a]) + (south + right))
            north = [s[0][b] * p[0] + s[1][b] * p[1] + s[2][b] * p[2] for b in range(3)]
            emit(r, p, cv)
            p = nxt

    def force(r, v, cv, th):
        inv, e = DI[at(r), :], E[at(r), :]
        return [
            inv * (th * raw[F0 + a, at(r), :] - e * v[a] - cv[a]) for a in range(3)
        ]

    def fine_tick(t):
        h = TICK

        def load(k, r, c):
            return U[k, span(r, c), :]

        def store_s(r, c, x):
            U[3, span(r, c), :] = x

        creep(load, store_s, t, h, 1, ROWS - 2, 8)
        th = h * t

        def first(r, v, cv):
            g = force(r, v, cv, th)
            for a in range(3):
                z = g[a] - (1.0 - MASS) * v[a]
                Z[a, at(r), :] = z
                Pd[a, at(r), :] = z
                if OWN <= r < OWN + 8:
                    U[a, at(r), :] = v[a] + z

        stencil(lambda b, r: U[b, at(r), :], 2, ROWS - 2, first)
        for k, (alpha, beta) in enumerate(chebyshev_weights()):
            def sweep(r, v, cv, alpha=alpha, beta=beta, k=k):
                inv = DI[at(r), :]
                for a in range(3):
                    z = Z[a, at(r), :] - v[a] - inv * cv[a]
                    p = alpha * v[a] + beta * z
                    if k < SWEEPS - 2:
                        Z[a, at(r), :] = z
                        Pd[a, at(r), :] = p
                    if OWN <= r < OWN + 8:
                        U[a, at(r), :] = U[a, at(r), :] + p

            stencil(lambda b, r: Pd[b, at(r), :], 3 + k, ROWS - 3 - k, sweep)

    def exchange(slot, sem, planes, between=None):
        own = U.at[pl.ds(0, planes), span(OWN, 8), :]
        pair = [
            copy(own, XH.at[slot, 0, pl.ds(0, planes)], sem, (n, dn)),
            copy(own, XH.at[slot, 1, pl.ds(0, planes)], sem + 1, (n, up)),
        ]
        for c in pair:
            c.start()
        if between is not None:
            between()
        for c in pair:
            c.wait()
        for k in range(planes):
            U[k, span(ABOVE, 8), :] = XH[slot, 0, k]
            U[k, span(BELOW, 8), :] = XH[slot, 1, k]

    def coarse_own():
        t = mean_heat(n)

        def load(k, r, c):
            return U[k, span(r, c), :]

        def store_s(r, c, x):
            GU[3, span(r - OWN, c), :] = x

        creep(load, store_s, t, 2.0 * TICK, OWN, 8, 8)

        def emit(r, v, cv):
            g = force(r, v, cv, 2.0 * TICK * t)
            for a in range(3):
                GU[a, at(r - OWN), :] = MASS * v[a] + g[a]

        stencil(lambda b, r: U[b, at(r), :], OWN, OWN + 8, emit)

    def coarse_step(m, _):
        t = mean_heat(m)

        def load(k, r, c):
            return U[k, span(r, c), :]

        def store_s(r, c, x):
            U[3, span(r, c), :] = x

        creep(load, store_s, t, 2.0 * TICK, 1, ROWS - 2, 8)

        def emit(r, v, cv):
            g = force(r, v, cv, 2.0 * TICK * t)
            for a in range(3):
                U[a, at(r), :] = MASS * v[a] + g[a]

        stencil(lambda b, r: U[b, at(r), :], 1, ROWS - 1, emit)
        return 0

    lax.fori_loop(0, n, coarse_step, 0)

    @pl.when(n == 1)
    def _():
        coarse_own()

    @pl.when(n > 1)
    def _():
        exchange(0, 15, 4, coarse_own)

    odd = lax.rem(n, 2) == 1
    even = (lax.rem(n, 2) == 0) & (n > 0)

    def to_next(p, rows):
        nxt = lax.rem(n + 1, n_tm)
        base = 23 + 6 * p
        top, low = span(0, rows), span(8 - rows, rows)
        return [
            copy(VOUT.at[p], VIN.at[p, :, span(OWN, 8), :], base, (nxt, sp)),
            copy(VOUT.at[p, :, top, :], VIN.at[p, :, span(BELOW, rows), :], base + 1, (nxt, up)),
            copy(VOUT.at[p, :, low, :], VIN.at[p, :, span(OWN - rows, rows), :], base + 2, (nxt, dn)),
        ]

    def to_second(p):
        nxt = lax.rem(n + 2, n_tm)
        base = 26 + 6 * p
        top, low = span(0, 2), span(6, 2)
        return [
            copy(VOUT.at[p, :, top, :], VIN.at[p, :, span(BELOW, 2), :], base + 1, (nxt, up)),
            copy(VOUT.at[p, :, low, :], VIN.at[p, :, span(OWN - 2, 2), :], base + 2, (nxt, dn)),
            copy(VOUT.at[p], VIN.at[p, :, span(OWN, 8), :], base, (nxt, sp)),
        ]

    def corrections(p):
        nxt = lax.rem(n + 1, n_tm)
        base = 35 + 3 * p
        top, low = span(0, 1), span(7, 1)
        return [
            copy(C.at[p, :, top, :], CIN.at[p, :, span(BELOW, 1), :], base + 1, (nxt, up)),
            copy(C.at[p, :, low, :], CIN.at[p, :, span(OWN - 1, 1), :], base + 2, (nxt, dn)),
            copy(C.at[p], CIN.at[p, :, span(OWN, 8), :], base, (nxt, sp)),
        ]

    def one_pass(p, _):
        @pl.when((n > 0) | (p == 0))
        def _():
            def tick(i, _):
                @pl.when(i == 1)
                def _():
                    exchange(1 + 2 * p, 17 + 4 * p, 3)

                fine_tick(heat_of(n, i))
                return 0

            lax.fori_loop(0, 2, tick, 0)

        @pl.when(n > 0)
        def _():
            for a in range(3):
                C[p, a] = U[a, span(OWN, 8), :] - GU[a]
            C[p, 3] = U[3, span(OWN, 8), :] / GU[3]

        @pl.when(odd & (n < n_tm - 1))
        def _():
            for c in corrections(p):
                c.start()

        @pl.when(odd & (p == 0))
        def _():
            for c in to_next(p, 8):
                c.wait_recv()
            for k in range(4):
                for r in (ABOVE, OWN, BELOW):
                    U[k, span(r, 8), :] = VIN[p, k, span(r, 8), :]

        @pl.when(odd & (p == 1))
        def _():
            for c in to_next(p, 1):
                c.wait_recv()
            for k in range(4):
                for r in range(OWN - 1, OWN + 9):
                    U[k, at(r), :] = VIN[p, k, at(r), :]

        @pl.when(even)
        def _():
            for c in to_second(p):
                c.wait_recv()
            for c in corrections(p):
                c.wait_recv()
            t = mean_heat(n - 1)

            def load(k, r, c):
                return VIN[p, k, span(r, c), :]

            def store_s(r, c, x):
                U[3, span(r, c), :] = x * CIN[p, 3, span(r, c), :]

            creep(load, store_s, t, 2.0 * TICK, OWN - 1, 10, 10)

            def emit(r, v, cv):
                g = force(r, v, cv, 2.0 * TICK * t)
                for a in range(3):
                    U[a, at(r), :] = MASS * v[a] + g[a] + CIN[p, a, at(r), :]

            stencil(lambda b, r: VIN[p, b, at(r), :], OWN - 1, OWN + 9, emit)

        @pl.when(n == 0)
        def _():
            for k in range(4):
                VOUT[p, k] = U[k, span(OWN, 8), :]

        @pl.when(n > 0)
        def _():
            coarse_own()
            for a in range(3):
                VOUT[p, a] = GU[a] + C[p, a]
            VOUT[p, 3] = GU[3] * C[p, 3]

        @pl.when(jnp.logical_not(odd) & (n < n_tm - 2))
        def _():
            for c in to_second(p):
                c.start()

        for q, rows in ((0, 8), (1, 1)):
            @pl.when(jnp.logical_not(odd) & (p == q))
            def _():
                for c in to_next(q, rows):
                    c.start()

        @pl.when(even & (p == 0))
        def _():
            exchange(2, 19, 4)

        return 0

    lax.fori_loop(0, 2, one_pass, 0)

    for c in range(8):
        cols = pl.ds(128 * c, 128)
        for a in range(3):
            u_out[0, a, :, cols] = VOUT[1, a, pl.ds(c, 8, stride=8), :]
        s_out[0, :, cols] = VOUT[1, 3, pl.ds(c, 8, stride=8), :]

    for p in range(2):
        @pl.when(odd & (n < n_tm - 1))
        def _():
            for c in corrections(p):
                c.wait_send()

        @pl.when(jnp.logical_not(odd))
        def _():
            for c in to_next(p, (8, 1)[p]):
                c.wait_send()

        @pl.when(jnp.logical_not(odd) & (n < n_tm - 2))
        def _():
            for c in to_second(p):
                c.wait_send()


def per_device(n_tm, n_sp, u, s, d, f, down, lat, heat, look):
    vmem = pl.BlockSpec(memory_space=pltpu.VMEM)
    hbm = pl.BlockSpec(memory_space=pl.ANY)
    f32 = jnp.float32
    inputs = (u, s, d, f, down, lat)
    return pl.pallas_call(
        functools.partial(kernel, n_tm, n_sp),
        out_shape=(
            jax.ShapeDtypeStruct((1, 3, 8, 1024), f32),
            jax.ShapeDtypeStruct((1, 8, 1024), f32),
        ),
        in_specs=[hbm] * 8,
        out_specs=(vmem, vmem),
        scratch_shapes=[pltpu.VMEM(x.shape, f32) for x in inputs] + [
            pltpu.SMEM(heat.shape, f32),
            pltpu.SMEM(look.shape, jnp.int32),
            pltpu.VMEM((PLANES, 8 * ROWS, 128), f32),
            pltpu.VMEM((8 * ROWS, 128), f32),
            pltpu.VMEM((4, 8 * ROWS, 128), f32),
            pltpu.VMEM((3, 8 * ROWS, 128), f32),
            pltpu.VMEM((3, 8 * ROWS, 128), f32),
            pltpu.VMEM((8 * ROWS, 128), f32),
            pltpu.VMEM((4, 64, 128), f32),
            pltpu.VMEM((2, 4, 64, 128), f32),
            pltpu.VMEM((2, 4, 64, 128), f32),
            pltpu.VMEM((2, 4, 8 * ROWS, 128), f32),
            pltpu.VMEM((2, 4, 8 * ROWS, 128), f32),
            pltpu.VMEM((4, 2, 4, 64, 128), f32),
            pltpu.VMEM((8, 16, 128), f32),
            pltpu.SemaphoreType.DMA((8,)),
            pltpu.SemaphoreType.DMA((41,)),
            pltpu.SemaphoreType.DMA((41,)),
        ],
        compiler_params=pltpu.CompilerParams(
            collective_id=0, has_side_effects=True, vmem_limit_bytes=60 * 1024 * 1024
        ),
        name="parareal",
    )(u, s, d, f, down, lat, heat, look)


def solution(mesh):
    return jax.shard_map(
        functools.partial(per_device, mesh.shape["tm"], mesh.shape["space"]),
        mesh=mesh,
        in_specs=(
            P(None, "space", None),
            P("space", None),
            P("space", None),
            P(None, "space", None),
            P(None, None, "space", None),
            P(None, None, "space", None),
            P(),
            P("tm"),
        ),
        out_specs=(P("tm", None, "space", None), P("tm", "space", None)),
        check_vma=False,
    )
```

```python
import functools

import jax
import jax.numpy as jnp
from jax import lax
from jax.experimental import pallas as pl
from jax.experimental.pallas import tpu as pltpu
from jax.sharding import PartitionSpec as P

COUPLING = 0.9 / 6.4
MASS = 0.3
HARDENING = 0.25
SATURATION = 3.0
TICK = 0.5
HALF_WIDTH = 0.9
SWEEPS = 8
ANAND = 4
ROWS = 26
OWN = 9
ABOVE, BELOW = 1, 17
PLANES = 26
S0, D0, U0, F0, L0 = 0, 9, 10, 14, 17
MESH = pl.DeviceIdType.MESH


def chebyshev_weights():
    weights, w = [], HALF_WIDTH
    for _ in range(SWEEPS - 1):
        nxt = 1.0 / (2.0 / HALF_WIDTH - w)
        weights.append((nxt * w, 2.0 * nxt / HALF_WIDTH))
        w = nxt
    return weights


def at(row):
    if isinstance(row, int):
        return pl.ds(8 * row, 8)
    return pl.ds(pl.multiple_of(8 * row, 8), 8)


def span(row, count):
    if isinstance(row, int):
        return pl.ds(8 * row, 8 * count)
    return pl.ds(pl.multiple_of(8 * row, 8), 8 * count)


def kernel(
    n_tm, n_sp,
    u_hbm, s_hbm, d_hbm, f_hbm, down_hbm, lat_hbm, heat_hbm, look_hbm,
    u_out, s_out,
    u_in, s_in, d_in, f_in, down_in, lat_in, heat, look,
    raw, DI, U, W, Pd, Z, E, GU, C, VOUT, VIN, CIN, XH, TH, lsem, ssem, rsem,
):
    n = lax.axis_index("tm")
    sp = lax.axis_index("space")
    up, dn = lax.rem(sp + n_sp - 1, n_sp), lax.rem(sp + 1, n_sp)
    up2, dn2 = lax.rem(sp + n_sp - 2, n_sp), lax.rem(sp + 2, n_sp)
    lane = lax.broadcasted_iota(jnp.int32, (8, 128), 1)
    sub = lax.broadcasted_iota(jnp.int32, (8, 128), 0)
    first_lane, last_lane = lane == 0, lane == 127

    loads = [
        pltpu.make_async_copy(src, dst, lsem.at[k])
        for k, (src, dst) in enumerate(
            [(look_hbm, look), (heat_hbm, heat), (down_hbm, down_in), (lat_hbm, lat_in),
             (u_hbm, u_in), (s_hbm, s_in), (d_hbm, d_in), (f_hbm, f_in)]
        )
    ]
    for c in loads:
        c.start()

    barrier = pltpu.get_barrier_semaphore()
    peers = [(lax.rem(n + d, n_tm), sp) for d in range(1, n_tm)]
    for d in (0, 1, 2, 3, n_tm - 3, n_tm - 2, n_tm - 1):
        for side in (up, dn):
            peers.append((lax.rem(n + d, n_tm), side))
    peers += [(n, up2), (n, dn2)]
    for peer in peers:
        pl.semaphore_signal(barrier, inc=1, device_id=peer, device_id_type=MESH)

    def copy(src, dst, sem, who):
        return pltpu.make_async_remote_copy(
            src_ref=src, dst_ref=dst, send_sem=ssem.at[sem], recv_sem=rsem.at[sem],
            device_id=who, device_id_type=MESH,
        )

    def pack(plane, tile_of):
        for c in range(8):
            raw[plane, pl.ds(8 * OWN + c, 8, stride=8), :] = tile_of(pl.ds(128 * c, 128))

    for c in loads:
        c.wait()
    for a in range(3):
        for b in range(3):
            pack(S0 + 3 * a + b, lambda cols, a=a, b=b: down_in[a, b, :, cols])
            pack(L0 + 3 * a + b, lambda cols, a=a, b=b: lat_in[a, b, :, cols])
        pack(F0 + a, lambda cols, a=a: f_in[a, :, cols])
        pack(U0 + a, lambda cols, a=a: u_in[a, :, cols])
    pack(D0, lambda cols: d_in[:, cols])
    pack(U0 + 3, lambda cols: s_in[:, cols])
    for k in range(2):
        TH[n, pl.ds(8 * k, 8), :] = jnp.full((8, 128), heat[look[k]], jnp.float32)

    pl.semaphore_wait(barrier, len(peers))

    core = lax.rem(sp, 2)
    y = n // 2
    sibling = sp + 1 - 2 * core
    outer = jnp.where(core == 0, up, dn)
    to_sibling = jnp.where(core == 0, ABOVE, BELOW)
    to_outer = jnp.where(core == 0, BELOW, ABOVE)
    from_outer = jnp.where(core == 0, ABOVE, BELOW)
    across = (n + 1 - 2 * lax.rem(n, 2), outer)
    shared = copy(raw.at[:, span(OWN + y, 1), :], raw.at[:, span(to_outer + y, 1), :], 1, across)
    shared.start()
    straight = [
        copy(raw.at[:, span(OWN + 4, 4), :], raw.at[:, span(to_outer + 4, 4), :], 2, across),
        copy(raw.at[:, span(OWN, 8), :], raw.at[:, span(to_sibling, 8), :], 0, (n, sibling)),
        copy(
            raw.at[pl.ds(0, F0 - 1), span(OWN + 7, 1), :],
            raw.at[pl.ds(0, F0 - 1), span(0, 1), :], 6, (n, dn2),
        ),
        copy(
            raw.at[pl.ds(D0, 4), span(OWN, 1), :],
            raw.at[pl.ds(D0, 4), span(ROWS - 1, 1), :], 7, (n, up2),
        ),
    ]
    heats = [
        copy(TH.at[n], TH.at[n], 7 + d, (lax.rem(n + d, n_tm), sp)) for d in range(1, n_tm)
    ]
    for c in straight + heats:
        c.start()
    shared.wait_recv()
    passed = raw.at[:, span(from_outer + y, 1), :]
    passing = [
        copy(passed, passed, 2 + d, (lax.rem(n + 2 * d, n_tm), sp)) for d in (1, 2, 3)
    ]
    for c in passing:
        c.start()
    for d in range(1, n_tm):
        src = lax.rem(n + n_tm - d, n_tm)
        copy(TH.at[src], TH.at[src], 7 + d, (src, sp)).wait_recv()
    for c in straight:
        c.wait()
    for d in (1, 2, 3):
        src = lax.rem(n + n_tm - 2 * d, n_tm)
        row = raw.at[:, span(from_outer + src // 2, 1), :]
        copy(row, row, 2 + d, (src, sp)).wait_recv()
    shared.wait_send()
    for c in heats + passing:
        c.wait_send()

    def east(v):
        a = pltpu.roll(v, 127, 1)
        return jnp.where(last_lane, pltpu.roll(a, 7, 0), a)

    def west(v):
        a = pltpu.roll(v, 1, 1)
        return jnp.where(first_lane, pltpu.roll(a, 1, 0), a)

    corner = (lane == 127) & (sub == 7)
    for r in range(ROWS):
        diag = raw[D0, at(r), :]
        if r < ROWS - 1:
            row = 8 * sp + (r - OWN)
            seam = (row == -1) | (row == 8 * n_sp - 1)
            below = raw[D0, at(r + 1), :]
            cs = COUPLING * jnp.minimum(diag, below) * jnp.where(seam, 0.0, 1.0)
            for k in range(9):
                raw[S0 + k, at(r), :] = raw[S0 + k, at(r), :] * cs
        if 0 < r < ROWS - 1:
            cl = jnp.where(corner, 0.0, COUPLING * jnp.minimum(diag, east(diag)))
            for k in range(9):
                raw[L0 + k, at(r), :] = raw[L0 + k, at(r), :] * cl
            DI[at(r), :] = 1.0 / diag
            U[3, at(r), :] = raw[U0 + 3, at(r), :]
        for k in range(3):
            U[k, at(r), :] = raw[U0 + k, at(r), :]

    def heat_of(slice_index, tick):
        return TH[slice_index, pl.ds(8 * tick, 1), :]

    def mean_heat(slice_index):
        return 0.5 * (TH[slice_index, 0:1, :] + TH[slice_index, 8:9, :])

    def creep(load, store_s, t, h, lo, count, chunk):
        rate = jnp.exp(2.0 - 2.0 / t)

        def body(i, _):
            r = lo + i * chunk
            u0, u1, u2, s = (load(k, r, chunk) for k in range(4))
            q2 = (u0 * u0 + u1 * u1 + u2 * u2) * (1.0 / 3.0) + 1.0
            qi = lax.rsqrt(q2)
            q = q2 * qi
            x = s
            for _ in range(ANAND):
                x = s + (h * HARDENING) * rate * jnp.tanh(q / x) * (1.0 - x * (1.0 / SATURATION))
            E[span(r, chunk), :] = (h * rate) * jnp.tanh(q / x) * qi
            store_s(r, chunk, x)
            return 0

        lax.fori_loop(0, count // chunk, body, 0)

    def stencil(load, lo, hi, emit):
        p = [load(b, lo - 1) for b in range(3)]
        s = [[raw[S0 + 3 * a + b, at(lo - 1), :] for b in range(3)] for a in range(3)]
        north = [s[0][b] * p[0] + s[1][b] * p[1] + s[2][b] * p[2] for b in range(3)]
        p = [load(b, lo) for b in range(3)]
        for r in range(lo, hi):
            nxt = [load(b, r + 1) for b in range(3)]
            s = [[raw[S0 + 3 * a + b, at(r), :] for b in range(3)] for a in range(3)]
            l = [[raw[L0 + 3 * a + b, at(r), :] for b in range(3)] for a in range(3)]
            pe = [east(p[b]) for b in range(3)]
            wf = [west(l[0][b] * p[0] + l[1][b] * p[1] + l[2][b] * p[2]) for b in range(3)]
            cv = []
            for a in range(3):
                south = s[a][0] * nxt[0] + s[a][1] * nxt[1] + s[a][2] * nxt[2]
                right = l[a][0] * pe[0] + l[a][1] * pe[1] + l[a][2] * pe[2]
                cv.append((north[a] + wf[a]) + (south + right))
            north = [s[0][b] * p[0] + s[1][b] * p[1] + s[2][b] * p[2] for b in range(3)]
            emit(r, p, cv)
            p = nxt

    def force(r, v, cv, th):
        inv, e = DI[at(r), :], E[at(r), :]
        return [
            inv * (th * raw[F0 + a, at(r), :] - e * v[a] - cv[a]) for a in range(3)
        ]

    def fine_tick(t):
        h = TICK

        def load(k, r, c):
            return U[k, span(r, c), :]

        def store_s(r, c, x):
            U[3, span(r, c), :] = x

        creep(load, store_s, t, h, 1, ROWS - 2, 8)
        th = h * t

        def first(r, v, cv):
            g = force(r, v, cv, th)
            for a in range(3):
                z = g[a] - (1.0 - MASS) * v[a]
                Z[a, at(r), :] = z
                Pd[a, at(r), :] = z
                if OWN <= r < OWN + 8:
                    U[a, at(r), :] = v[a] + z

        stencil(lambda b, r: U[b, at(r), :], 2, ROWS - 2, first)
        for k, (alpha, beta) in enumerate(chebyshev_weights()):
            def sweep(r, v, cv, alpha=alpha, beta=beta, k=k):
                inv = DI[at(r), :]
                for a in range(3):
                    z = Z[a, at(r), :] - v[a] - inv * cv[a]
                    p = alpha * v[a] + beta * z
                    if k < SWEEPS - 2:
                        Z[a, at(r), :] = z
                        Pd[a, at(r), :] = p
                    if OWN <= r < OWN + 8:
                        U[a, at(r), :] = U[a, at(r), :] + p

            stencil(lambda b, r: Pd[b, at(r), :], 3 + k, ROWS - 3 - k, sweep)

    def exchange(slot, sem, planes, between=None):
        own = U.at[pl.ds(0, planes), span(OWN, 8), :]
        pair = [
            copy(own, XH.at[slot, 0, pl.ds(0, planes)], sem, (n, dn)),
            copy(own, XH.at[slot, 1, pl.ds(0, planes)], sem + 1, (n, up)),
        ]
        for c in pair:
            c.start()
        if between is not None:
            between()
        for c in pair:
            c.wait()
        for k in range(planes):
            U[k, span(ABOVE, 8), :] = XH[slot, 0, k]
            U[k, span(BELOW, 8), :] = XH[slot, 1, k]

    def coarse_own():
        t = mean_heat(n)

        def load(k, r, c):
            return U[k, span(r, c), :]

        def store_s(r, c, x):
            GU[3, span(r - OWN, c), :] = x

        creep(load, store_s, t, 2.0 * TICK, OWN, 8, 8)

        def emit(r, v, cv):
            g = force(r, v, cv, 2.0 * TICK * t)
            for a in range(3):
                GU[a, at(r - OWN), :] = MASS * v[a] + g[a]

        stencil(lambda b, r: U[b, at(r), :], OWN, OWN + 8, emit)

    def coarse_step(m, _):
        t = mean_heat(m)

        def load(k, r, c):
            return U[k, span(r, c), :]

        def store_s(r, c, x):
            U[3, span(r, c), :] = x

        creep(load, store_s, t, 2.0 * TICK, 1, ROWS - 2, 8)

        def emit(r, v, cv):
            g = force(r, v, cv, 2.0 * TICK * t)
            for a in range(3):
                U[a, at(r), :] = MASS * v[a] + g[a]

        stencil(lambda b, r: U[b, at(r), :], 1, ROWS - 1, emit)
        return 0

    lax.fori_loop(0, n, coarse_step, 0)

    @pl.when(n == 1)
    def _():
        coarse_own()

    @pl.when(n > 1)
    def _():
        exchange(0, 15, 4, coarse_own)

    odd = lax.rem(n, 2) == 1
    sender = lax.rem(n, 2) == 0
    even = sender & (n > 0)

    def to_next(p, rows):
        nxt = lax.rem(n + 1, n_tm)
        base = 23 + 6 * p
        top, low = span(0, rows), span(8 - rows, rows)
        return [
            copy(VOUT.at[p], VIN.at[p, :, span(OWN, 8), :], base, (nxt, sp)),
            copy(VOUT.at[p, :, top, :], VIN.at[p, :, span(BELOW, rows), :], base + 1, (nxt, up)),
            copy(VOUT.at[p, :, low, :], VIN.at[p, :, span(OWN - rows, rows), :], base + 2, (nxt, dn)),
        ]

    def to_second(p):
        nxt = lax.rem(n + 2, n_tm)
        base = 26 + 6 * p
        top, low = span(0, 2), span(6, 2)
        return [
            copy(VOUT.at[p, :, top, :], VIN.at[p, :, span(BELOW, 2), :], base + 1, (nxt, up)),
            copy(VOUT.at[p, :, low, :], VIN.at[p, :, span(OWN - 2, 2), :], base + 2, (nxt, dn)),
            copy(VOUT.at[p], VIN.at[p, :, span(OWN, 8), :], base, (nxt, sp)),
        ]

    def corrections(p):
        nxt = lax.rem(n + 1, n_tm)
        base = 35 + 3 * p
        top, low = span(0, 1), span(7, 1)
        return [
            copy(C.at[p, :, top, :], CIN.at[p, :, span(BELOW, 1), :], base + 1, (nxt, up)),
            copy(C.at[p, :, low, :], CIN.at[p, :, span(OWN - 1, 1), :], base + 2, (nxt, dn)),
            copy(C.at[p], CIN.at[p, :, span(OWN, 8), :], base, (nxt, sp)),
        ]

    last = n_tm - 1

    def trimmed(src, dst, rows, base, who):
        return [
            copy(src.at[:, span(0, rows), :], dst.at[:, span(BELOW, rows), :], base + 1, (who, up)),
            copy(
                src.at[:, span(8 - rows, rows), :], dst.at[:, span(OWN - rows, rows), :],
                base + 2, (who, dn),
            ),
            copy(src, dst.at[:, span(OWN, 8), :], base, (who, sp)),
        ]

    def end_to_last():
        return trimmed(VOUT.at[1], VIN.at[1], 3, 41, last)

    def correction_to_last(back):
        if back == 2:
            return trimmed(C.at[1], CIN.at[1], 2, 44, last)
        return trimmed(C.at[1], CIN.at[0], 1, 47, last)

    def corrected(load, corr, dst, t, lo, count):
        def store_s(r, c, x):
            dst[3, span(r, c), :] = x * corr[3, span(r, c), :]

        creep(load, store_s, t, 2.0 * TICK, lo, count, count)

        def emit(r, v, cv):
            g = force(r, v, cv, 2.0 * TICK * t)
            for a in range(3):
                dst[a, at(r), :] = MASS * v[a] + g[a] + corr[a, at(r), :]

        stencil(lambda b, r: load(b, r, 1), lo, lo + count, emit)

    def one_pass(p, _):
        @pl.when((n > 0) | (p == 0))
        def _():
            def tick(i, _):
                @pl.when(i == 1)
                def _():
                    exchange(1 + 2 * p, 17 + 4 * p, 3)

                fine_tick(heat_of(n, i))
                return 0

            lax.fori_loop(0, 2, tick, 0)

        @pl.when(n > 0)
        def _():
            for a in range(3):
                C[p, a] = U[a, span(OWN, 8), :] - GU[a]
            C[p, 3] = U[3, span(OWN, 8), :] / GU[3]

        @pl.when(odd & (n < n_tm - 1))
        def _():
            for c in corrections(p):
                c.start()

        @pl.when(odd & (p == 0))
        def _():
            for c in to_next(p, 8):
                c.wait_recv()
            for k in range(4):
                for r in (ABOVE, OWN, BELOW):
                    U[k, span(r, 8), :] = VIN[p, k, span(r, 8), :]

        for back in (2, 1):
            @pl.when((n == last - back) & (p == 1))
            def _():
                for c in correction_to_last(back):
                    c.start()

        @pl.when((n == last) & (p == 1))
        def _():
            for c in end_to_last() + correction_to_last(2) + correction_to_last(1):
                c.wait_recv()
            corrected(
                lambda k, r, c: VIN[1, k, span(r, c), :], CIN.at[1], W,
                mean_heat(last - 2), OWN - 2, 12,
            )
            corrected(
                lambda k, r, c: W[k, span(r, c), :], CIN.at[0], U,
                mean_heat(last - 1), OWN - 1, 10,
            )

        @pl.when(odd & (n < last) & (p == 1))
        def _():
            @pl.when(n > 1)
            def _():
                for c in to_next(p, 1):
                    c.wait_recv()

            q = jnp.where(n == 1, 0, p)
            for k in range(4):
                for r in range(OWN - 1, OWN + 9):
                    U[k, at(r), :] = VIN[q, k, at(r), :]

        @pl.when(even)
        def _():
            @pl.when((n > 2) | (p == 0))
            def _():
                for c in to_second(p):
                    c.wait_recv()

            for c in corrections(p):
                c.wait_recv()
            q = jnp.where(n == 2, 0, p)
            corrected(
                lambda k, r, c: VIN[q, k, span(r, c), :], CIN.at[p], U,
                mean_heat(n - 1), OWN - 1, 10,
            )

        @pl.when(n == 0)
        def _():
            for k in range(4):
                VOUT[p, k] = U[k, span(OWN, 8), :]

        def pass_on():
            @pl.when(n > 0)
            def _():
                coarse_own()
                for a in range(3):
                    VOUT[p, a] = GU[a] + C[p, a]
                VOUT[p, 3] = GU[3] * C[p, 3]

            @pl.when(sender & (n < n_tm - 2) & ((n > 0) | (p == 0)))
            def _():
                for c in to_second(p):
                    c.start()

            @pl.when((n == last - 3) & (p == 1))
            def _():
                for c in end_to_last():
                    c.start()

            for q, rows in ((0, 8), (1, 1)):
                @pl.when(sender & (p == q) & (((n > 0) & (n < last - 1)) | (p == 0)))
                def _():
                    for c in to_next(q, rows):
                        c.start()

        halo_now = even & (p == 0)

        @pl.when(halo_now)
        def _():
            exchange(2, 19, 4, pass_on)

        @pl.when(jnp.logical_not(halo_now))
        def _():
            pass_on()

        return 0

    lax.fori_loop(0, 2, one_pass, 0)

    for c in range(8):
        cols = pl.ds(128 * c, 128)
        for a in range(3):
            u_out[0, a, :, cols] = VOUT[1, a, pl.ds(c, 8, stride=8), :]
        s_out[0, :, cols] = VOUT[1, 3, pl.ds(c, 8, stride=8), :]

    for p in range(2):
        @pl.when(odd & (n < n_tm - 1))
        def _():
            for c in corrections(p):
                c.wait_send()

        @pl.when(sender & (((n > 0) & (n < last - 1)) | (p == 0)))
        def _():
            for c in to_next(p, (8, 1)[p]):
                c.wait_send()

        @pl.when(sender & (n < n_tm - 2) & ((n > 0) | (p == 0)))
        def _():
            for c in to_second(p):
                c.wait_send()

    @pl.when(n == last - 3)
    def _():
        for c in end_to_last():
            c.wait_send()

    for back in (2, 1):
        @pl.when(n == last - back)
        def _():
            for c in correction_to_last(back):
                c.wait_send()


def per_device(n_tm, n_sp, u, s, d, f, down, lat, heat, look):
    vmem = pl.BlockSpec(memory_space=pltpu.VMEM)
    hbm = pl.BlockSpec(memory_space=pl.ANY)
    f32 = jnp.float32
    inputs = (u, s, d, f, down, lat)
    return pl.pallas_call(
        functools.partial(kernel, n_tm, n_sp),
        out_shape=(
            jax.ShapeDtypeStruct((1, 3, 8, 1024), f32),
            jax.ShapeDtypeStruct((1, 8, 1024), f32),
        ),
        in_specs=[hbm] * 8,
        out_specs=(vmem, vmem),
        scratch_shapes=[pltpu.VMEM(x.shape, f32) for x in inputs] + [
            pltpu.SMEM(heat.shape, f32),
            pltpu.SMEM(look.shape, jnp.int32),
            pltpu.VMEM((PLANES, 8 * ROWS, 128), f32),
            pltpu.VMEM((8 * ROWS, 128), f32),
            pltpu.VMEM((4, 8 * ROWS, 128), f32),
            pltpu.VMEM((4, 8 * ROWS, 128), f32),
            pltpu.VMEM((3, 8 * ROWS, 128), f32),
            pltpu.VMEM((3, 8 * ROWS, 128), f32),
            pltpu.VMEM((8 * ROWS, 128), f32),
            pltpu.VMEM((4, 64, 128), f32),
            pltpu.VMEM((2, 4, 64, 128), f32),
            pltpu.VMEM((2, 4, 64, 128), f32),
            pltpu.VMEM((2, 4, 8 * ROWS, 128), f32),
            pltpu.VMEM((2, 4, 8 * ROWS, 128), f32),
            pltpu.VMEM((4, 2, 4, 64, 128), f32),
            pltpu.VMEM((8, 16, 128), f32),
            pltpu.SemaphoreType.DMA((8,)),
            pltpu.SemaphoreType.DMA((50,)),
            pltpu.SemaphoreType.DMA((50,)),
        ],
        compiler_params=pltpu.CompilerParams(
            collective_id=0, has_side_effects=True, vmem_limit_bytes=60 * 1024 * 1024
        ),
        name="parareal",
    )(u, s, d, f, down, lat, heat, look)


def solution(mesh):
    return jax.shard_map(
        functools.partial(per_device, mesh.shape["tm"], mesh.shape["space"]),
        mesh=mesh,
        in_specs=(
            P(None, "space", None),
            P("space", None),
            P("space", None),
            P(None, "space", None),
            P(None, None, "space", None),
            P(None, None, "space", None),
            P(),
            P("tm"),
        ),
        out_specs=(P("tm", None, "space", None), P("tm", "space", None)),
        check_vma=False,
    )
```

```python
import functools

import jax
import jax.numpy as jnp
from jax import lax
from jax.experimental import pallas as pl
from jax.experimental.pallas import tpu as pltpu
from jax.sharding import PartitionSpec as P

COUPLING = 0.9 / 6.4
MASS = 0.3
HARDENING = 0.25
SATURATION = 3.0
TICK = 0.5
HALF_WIDTH = 0.9
SWEEPS = 8
ANAND = 4
ROWS = 26
OWN = 9
ABOVE, BELOW = 1, 17
PLANES = 26
S0, D0, U0, F0, L0 = 0, 9, 10, 14, 17
MESH = pl.DeviceIdType.MESH


def chebyshev_weights():
    weights, w = [], HALF_WIDTH
    for _ in range(SWEEPS - 1):
        nxt = 1.0 / (2.0 / HALF_WIDTH - w)
        weights.append((nxt * w, 2.0 * nxt / HALF_WIDTH))
        w = nxt
    return weights


def at(row):
    if isinstance(row, int):
        return pl.ds(8 * row, 8)
    return pl.ds(pl.multiple_of(8 * row, 8), 8)


def span(row, count):
    if isinstance(row, int):
        return pl.ds(8 * row, 8 * count)
    return pl.ds(pl.multiple_of(8 * row, 8), 8 * count)


def kernel(
    n_tm, n_sp,
    u_hbm, s_hbm, d_hbm, f_hbm, down_hbm, lat_hbm, heat_hbm, look_hbm,
    u_out, s_out,
    u_in, s_in, d_in, f_in, down_in, lat_in, heat, look,
    raw, DI, U, Pd, Z, E, GU, C, VOUT, VIN, CIN, XH, TH, lsem, ssem, rsem,
):
    n = lax.axis_index("tm")
    sp = lax.axis_index("space")
    up, dn = lax.rem(sp + n_sp - 1, n_sp), lax.rem(sp + 1, n_sp)
    up2, dn2 = lax.rem(sp + n_sp - 2, n_sp), lax.rem(sp + 2, n_sp)
    lane = lax.broadcasted_iota(jnp.int32, (8, 128), 1)
    sub = lax.broadcasted_iota(jnp.int32, (8, 128), 0)
    first_lane, last_lane = lane == 0, lane == 127

    loads = [
        pltpu.make_async_copy(src, dst, lsem.at[k])
        for k, (src, dst) in enumerate(
            [(look_hbm, look), (heat_hbm, heat), (down_hbm, down_in), (lat_hbm, lat_in),
             (u_hbm, u_in), (s_hbm, s_in), (d_hbm, d_in), (f_hbm, f_in)]
        )
    ]
    for c in loads:
        c.start()

    barrier = pltpu.get_barrier_semaphore()
    peers = [(lax.rem(n + d, n_tm), sp) for d in range(1, n_tm)]
    for d in (0, 1, 2, n_tm - 2, n_tm - 1):
        for side in (up, dn):
            peers.append((lax.rem(n + d, n_tm), side))
    peers += [(n, up2), (n, dn2)]
    for peer in peers:
        pl.semaphore_signal(barrier, inc=1, device_id=peer, device_id_type=MESH)

    def copy(src, dst, sem, who):
        return pltpu.make_async_remote_copy(
            src_ref=src, dst_ref=dst, send_sem=ssem.at[sem], recv_sem=rsem.at[sem],
            device_id=who, device_id_type=MESH,
        )

    def pack(plane, tile_of):
        for c in range(8):
            raw[plane, pl.ds(8 * OWN + c, 8, stride=8), :] = tile_of(pl.ds(128 * c, 128))

    for c in loads:
        c.wait()
    for a in range(3):
        for b in range(3):
            pack(S0 + 3 * a + b, lambda cols, a=a, b=b: down_in[a, b, :, cols])
            pack(L0 + 3 * a + b, lambda cols, a=a, b=b: lat_in[a, b, :, cols])
        pack(F0 + a, lambda cols, a=a: f_in[a, :, cols])
        pack(U0 + a, lambda cols, a=a: u_in[a, :, cols])
    pack(D0, lambda cols: d_in[:, cols])
    pack(U0 + 3, lambda cols: s_in[:, cols])
    for k in range(2):
        TH[n, pl.ds(8 * k, 8), :] = jnp.full((8, 128), heat[look[k]], jnp.float32)

    pl.semaphore_wait(barrier, len(peers))

    core = lax.rem(sp, 2)
    y = n // 2
    sibling = sp + 1 - 2 * core
    outer = jnp.where(core == 0, up, dn)
    to_sibling = jnp.where(core == 0, ABOVE, BELOW)
    to_outer = jnp.where(core == 0, BELOW, ABOVE)
    from_outer = jnp.where(core == 0, ABOVE, BELOW)
    across = (n + 1 - 2 * lax.rem(n, 2), outer)
    shared = copy(raw.at[:, span(OWN + y, 1), :], raw.at[:, span(to_outer + y, 1), :], 1, across)
    shared.start()
    straight = [
        copy(raw.at[:, span(OWN + 4, 4), :], raw.at[:, span(to_outer + 4, 4), :], 2, across),
        copy(raw.at[:, span(OWN, 8), :], raw.at[:, span(to_sibling, 8), :], 0, (n, sibling)),
        copy(
            raw.at[pl.ds(0, F0 - 1), span(OWN + 7, 1), :],
            raw.at[pl.ds(0, F0 - 1), span(0, 1), :], 6, (n, dn2),
        ),
        copy(
            raw.at[pl.ds(D0, 4), span(OWN, 1), :],
            raw.at[pl.ds(D0, 4), span(ROWS - 1, 1), :], 7, (n, up2),
        ),
    ]
    heats = [
        copy(TH.at[n], TH.at[n], 7 + d, (lax.rem(n + d, n_tm), sp)) for d in range(1, n_tm)
    ]
    for c in straight + heats:
        c.start()
    shared.wait_recv()
    passed = raw.at[:, span(from_outer + y, 1), :]
    passing = [
        copy(passed, passed, 2 + d, (lax.rem(n + 2 * d, n_tm), sp)) for d in (1, 2, 3)
    ]
    for c in passing:
        c.start()
    for d in range(1, n_tm):
        src = lax.rem(n + n_tm - d, n_tm)
        copy(TH.at[src], TH.at[src], 7 + d, (src, sp)).wait_recv()
    for c in straight:
        c.wait()
    for d in (1, 2, 3):
        src = lax.rem(n + n_tm - 2 * d, n_tm)
        row = raw.at[:, span(from_outer + src // 2, 1), :]
        copy(row, row, 2 + d, (src, sp)).wait_recv()
    shared.wait_send()
    for c in heats + passing:
        c.wait_send()

    def east(v):
        a = pltpu.roll(v, 127, 1)
        return jnp.where(last_lane, pltpu.roll(a, 7, 0), a)

    def west(v):
        a = pltpu.roll(v, 1, 1)
        return jnp.where(first_lane, pltpu.roll(a, 1, 0), a)

    corner = (lane == 127) & (sub == 7)
    for r in range(ROWS):
        diag = raw[D0, at(r), :]
        if r < ROWS - 1:
            row = 8 * sp + (r - OWN)
            seam = (row == -1) | (row == 8 * n_sp - 1)
            below = raw[D0, at(r + 1), :]
            cs = COUPLING * jnp.minimum(diag, below) * jnp.where(seam, 0.0, 1.0)
            for k in range(9):
                raw[S0 + k, at(r), :] = raw[S0 + k, at(r), :] * cs
        if 0 < r < ROWS - 1:
            cl = jnp.where(corner, 0.0, COUPLING * jnp.minimum(diag, east(diag)))
            for k in range(9):
                raw[L0 + k, at(r), :] = raw[L0 + k, at(r), :] * cl
            DI[at(r), :] = 1.0 / diag
            U[3, at(r), :] = raw[U0 + 3, at(r), :]
        for k in range(3):
            U[k, at(r), :] = raw[U0 + k, at(r), :]

    def heat_of(slice_index, tick):
        return TH[slice_index, pl.ds(8 * tick, 1), :]

    def mean_heat(slice_index):
        return 0.5 * (TH[slice_index, 0:1, :] + TH[slice_index, 8:9, :])

    def creep(load, store_s, t, h, lo, count, chunk):
        rate = jnp.exp(2.0 - 2.0 / t)

        def body(i, _):
            r = lo + i * chunk
            u0, u1, u2, s = (load(k, r, chunk) for k in range(4))
            q2 = (u0 * u0 + u1 * u1 + u2 * u2) * (1.0 / 3.0) + 1.0
            qi = lax.rsqrt(q2)
            q = q2 * qi
            x = s
            for _ in range(ANAND):
                x = s + (h * HARDENING) * rate * jnp.tanh(q / x) * (1.0 - x * (1.0 / SATURATION))
            E[span(r, chunk), :] = (h * rate) * jnp.tanh(q / x) * qi
            store_s(r, chunk, x)
            return 0

        lax.fori_loop(0, count // chunk, body, 0)

    def stencil(load, lo, hi, emit):
        p = [load(b, lo - 1) for b in range(3)]
        s = [[raw[S0 + 3 * a + b, at(lo - 1), :] for b in range(3)] for a in range(3)]
        north = [s[0][b] * p[0] + s[1][b] * p[1] + s[2][b] * p[2] for b in range(3)]
        p = [load(b, lo) for b in range(3)]
        for r in range(lo, hi):
            nxt = [load(b, r + 1) for b in range(3)]
            s = [[raw[S0 + 3 * a + b, at(r), :] for b in range(3)] for a in range(3)]
            l = [[raw[L0 + 3 * a + b, at(r), :] for b in range(3)] for a in range(3)]
            pe = [east(p[b]) for b in range(3)]
            wf = [west(l[0][b] * p[0] + l[1][b] * p[1] + l[2][b] * p[2]) for b in range(3)]
            cv = []
            for a in range(3):
                south = s[a][0] * nxt[0] + s[a][1] * nxt[1] + s[a][2] * nxt[2]
                right = l[a][0] * pe[0] + l[a][1] * pe[1] + l[a][2] * pe[2]
                cv.append((north[a] + wf[a]) + (south + right))
            north = [s[0][b] * p[0] + s[1][b] * p[1] + s[2][b] * p[2] for b in range(3)]
            emit(r, p, cv)
            p = nxt

    def force(r, v, cv, th):
        inv, e = DI[at(r), :], E[at(r), :]
        return [
            inv * (th * raw[F0 + a, at(r), :] - e * v[a] - cv[a]) for a in range(3)
        ]

    def fine_tick(t):
        h = TICK

        def load(k, r, c):
            return U[k, span(r, c), :]

        def store_s(r, c, x):
            U[3, span(r, c), :] = x

        creep(load, store_s, t, h, 1, ROWS - 2, 8)
        th = h * t

        def first(r, v, cv):
            g = force(r, v, cv, th)
            for a in range(3):
                z = g[a] - (1.0 - MASS) * v[a]
                Z[a, at(r), :] = z
                Pd[a, at(r), :] = z
                if OWN <= r < OWN + 8:
                    U[a, at(r), :] = v[a] + z

        stencil(lambda b, r: U[b, at(r), :], 2, ROWS - 2, first)
        for k, (alpha, beta) in enumerate(chebyshev_weights()):
            def sweep(r, v, cv, alpha=alpha, beta=beta, k=k):
                inv = DI[at(r), :]
                for a in range(3):
                    z = Z[a, at(r), :] - v[a] - inv * cv[a]
                    p = alpha * v[a] + beta * z
                    if k < SWEEPS - 2:
                        Z[a, at(r), :] = z
                        Pd[a, at(r), :] = p
                    if OWN <= r < OWN + 8:
                        U[a, at(r), :] = U[a, at(r), :] + p

            stencil(lambda b, r: Pd[b, at(r), :], 3 + k, ROWS - 3 - k, sweep)

    def exchange(slot, sem, planes, between=None):
        own = U.at[pl.ds(0, planes), span(OWN, 8), :]
        pair = [
            copy(own, XH.at[slot, 0, pl.ds(0, planes)], sem, (n, dn)),
            copy(own, XH.at[slot, 1, pl.ds(0, planes)], sem + 1, (n, up)),
        ]
        for c in pair:
            c.start()
        if between is not None:
            between()
        for c in pair:
            c.wait()
        for k in range(planes):
            U[k, span(ABOVE, 8), :] = XH[slot, 0, k]
            U[k, span(BELOW, 8), :] = XH[slot, 1, k]

    def coarse_own():
        t = mean_heat(n)

        def load(k, r, c):
            return U[k, span(r, c), :]

        def store_s(r, c, x):
            GU[3, span(r - OWN, c), :] = x

        creep(load, store_s, t, 2.0 * TICK, OWN, 8, 8)

        def emit(r, v, cv):
            g = force(r, v, cv, 2.0 * TICK * t)
            for a in range(3):
                GU[a, at(r - OWN), :] = MASS * v[a] + g[a]

        stencil(lambda b, r: U[b, at(r), :], OWN, OWN + 8, emit)

    def coarse_step(m, _):
        t = mean_heat(m)

        def load(k, r, c):
            return U[k, span(r, c), :]

        def store_s(r, c, x):
            U[3, span(r, c), :] = x

        creep(load, store_s, t, 2.0 * TICK, 1, ROWS - 2, 8)

        def emit(r, v, cv):
            g = force(r, v, cv, 2.0 * TICK * t)
            for a in range(3):
                U[a, at(r), :] = MASS * v[a] + g[a]

        stencil(lambda b, r: U[b, at(r), :], 1, ROWS - 1, emit)
        return 0

    lax.fori_loop(0, n, coarse_step, 0)

    @pl.when(n == 1)
    def _():
        coarse_own()

    @pl.when(n > 1)
    def _():
        exchange(0, 15, 4, coarse_own)

    odd = lax.rem(n, 2) == 1
    even = (lax.rem(n, 2) == 0) & (n > 0)
    hands_on = odd & (n < n_tm - 1)
    joins = odd & (n > 1)

    def trimmed(src, dst, rows, base, who):
        return [
            copy(src.at[:, span(0, rows), :], dst.at[:, span(BELOW, rows), :], base + 1, (who, up)),
            copy(
                src.at[:, span(8 - rows, rows), :], dst.at[:, span(OWN - rows, rows), :],
                base + 2, (who, dn),
            ),
            copy(src, dst.at[:, span(OWN, 8), :], base, (who, sp)),
        ]

    def whole_halo(base, who):
        return copy(VOUT.at[0], VIN.at[0, :, span(to_outer, 8), :], base, (who, outer))

    def beside(slot):
        own = VIN.at[slot, :, span(OWN, 8), :]
        return copy(own, VIN.at[0, :, span(to_sibling, 8), :], 25, (n, sibling))

    def to_first():
        return trimmed(VOUT.at[0], VIN.at[1], 1, 41, 1) + [whole_halo(44, 1)]

    def to_next(p):
        nxt = lax.rem(n + 1, n_tm)
        if p == 0:
            own = copy(VOUT.at[0], VIN.at[0, :, span(OWN, 8), :], 23, (nxt, sp))
            return [own, whole_halo(24, nxt)]
        return trimmed(VOUT.at[1], VIN.at[1], 1, 29, nxt)

    def to_second(p):
        return trimmed(VOUT.at[p], VIN.at[p], 2, 26 + 6 * p, lax.rem(n + 2, n_tm))

    def corrections(p):
        return trimmed(C.at[p], CIN.at[p], 1, 35 + 3 * p, lax.rem(n + 1, n_tm))

    def corrected(load, corr, dst, t, lo, count):
        def store_s(r, c, x):
            dst[3, span(r, c), :] = x * corr[3, span(r, c), :]

        creep(load, store_s, t, 2.0 * TICK, lo, count, count)

        def emit(r, v, cv):
            g = force(r, v, cv, 2.0 * TICK * t)
            for a in range(3):
                dst[a, at(r), :] = MASS * v[a] + g[a] + corr[a, at(r), :]

        stencil(lambda b, r: load(b, r, 1), lo, lo + count, emit)

    def one_pass(p, _):
        @pl.when((n > 0) | (p == 0))
        def _():
            def tick(i, _):
                @pl.when(i == 1)
                def _():
                    exchange(1 + 2 * p, 17 + 4 * p, 3)

                fine_tick(heat_of(n, i))
                return 0

            lax.fori_loop(0, 2, tick, 0)

        @pl.when(n > 0)
        def _():
            for a in range(3):
                C[p, a] = U[a, span(OWN, 8), :] - GU[a]
            C[p, 3] = U[3, span(OWN, 8), :] / GU[3]

        @pl.when(even)
        def _():
            for c in corrections(p):
                c.start()

        @pl.when((n == 1) & (p == 0))
        def _():
            for c in to_first()[:3]:
                c.wait_recv()

        @pl.when(even & (p == 0))
        def _():
            own, halo = to_next(0)
            own.wait_recv()
            pair = beside(0)
            pair.start()
            pair.wait()
            halo.wait_recv()
            for k in range(4):
                for r in (ABOVE, OWN, BELOW):
                    U[k, span(r, 8), :] = VIN[0, k, span(r, 8), :]

        @pl.when(even & (p == 1))
        def _():
            for c in to_next(1):
                c.wait_recv()

        @pl.when((n == 1) | (even & (p == 1)))
        def _():
            for k in range(4):
                U[k, span(OWN - 1, 10), :] = VIN[1, k, span(OWN - 1, 10), :]

        @pl.when(joins)
        def _():
            for c in corrections(p):
                c.wait_recv()
            for c in to_second(p):
                c.wait_recv()
            corrected(
                lambda k, r, c: VIN[p, k, span(r, c), :], CIN.at[p], U,
                mean_heat(n - 1), OWN - 1, 10,
            )

        @pl.when(n == 0)
        def _():
            for k in range(4):
                VOUT[p, k] = U[k, span(OWN, 8), :]

        def pass_on():
            @pl.when(n > 0)
            def _():
                coarse_own()
                for a in range(3):
                    VOUT[p, a] = GU[a] + C[p, a]
                VOUT[p, 3] = GU[3] * C[p, 3]

            @pl.when((n == 0) & (p == 0))
            def _():
                for c in to_first():
                    c.start()

            @pl.when(hands_on)
            def _():
                for c in to_second(p):
                    c.start()

            for q in range(2):
                @pl.when(hands_on & (p == q))
                def _():
                    for c in to_next(q):
                        c.start()

        halo_now = joins & (p == 0)

        @pl.when(halo_now)
        def _():
            exchange(2, 19, 4, pass_on)

        @pl.when(jnp.logical_not(halo_now))
        def _():
            pass_on()

        @pl.when((n == 1) & (p == 0))
        def _():
            pair = beside(1)
            pair.start()
            pair.wait()
            to_first()[3].wait_recv()
            for k in range(4):
                for r in (ABOVE, BELOW):
                    U[k, span(r, 8), :] = VIN[0, k, span(r, 8), :]

        return 0

    lax.fori_loop(0, 2, one_pass, 0)

    for c in range(8):
        cols = pl.ds(128 * c, 128)
        for a in range(3):
            u_out[0, a, :, cols] = VOUT[1, a, pl.ds(c, 8, stride=8), :]
        s_out[0, :, cols] = VOUT[1, 3, pl.ds(c, 8, stride=8), :]

    @pl.when(n == 0)
    def _():
        for c in to_first():
            c.wait_send()

    for p in range(2):
        @pl.when(even)
        def _():
            for c in corrections(p):
                c.wait_send()

        @pl.when(hands_on)
        def _():
            for c in to_next(p) + to_second(p):
                c.wait_send()


def per_device(n_tm, n_sp, u, s, d, f, down, lat, heat, look):
    vmem = pl.BlockSpec(memory_space=pltpu.VMEM)
    hbm = pl.BlockSpec(memory_space=pl.ANY)
    f32 = jnp.float32
    inputs = (u, s, d, f, down, lat)
    return pl.pallas_call(
        functools.partial(kernel, n_tm, n_sp),
        out_shape=(
            jax.ShapeDtypeStruct((1, 3, 8, 1024), f32),
            jax.ShapeDtypeStruct((1, 8, 1024), f32),
        ),
        in_specs=[hbm] * 8,
        out_specs=(vmem, vmem),
        scratch_shapes=[pltpu.VMEM(x.shape, f32) for x in inputs] + [
            pltpu.SMEM(heat.shape, f32),
            pltpu.SMEM(look.shape, jnp.int32),
            pltpu.VMEM((PLANES, 8 * ROWS, 128), f32),
            pltpu.VMEM((8 * ROWS, 128), f32),
            pltpu.VMEM((4, 8 * ROWS, 128), f32),
            pltpu.VMEM((3, 8 * ROWS, 128), f32),
            pltpu.VMEM((3, 8 * ROWS, 128), f32),
            pltpu.VMEM((8 * ROWS, 128), f32),
            pltpu.VMEM((4, 64, 128), f32),
            pltpu.VMEM((2, 4, 64, 128), f32),
            pltpu.VMEM((2, 4, 64, 128), f32),
            pltpu.VMEM((2, 4, 8 * ROWS, 128), f32),
            pltpu.VMEM((2, 4, 8 * ROWS, 128), f32),
            pltpu.VMEM((4, 2, 4, 64, 128), f32),
            pltpu.VMEM((8, 16, 128), f32),
            pltpu.SemaphoreType.DMA((8,)),
            pltpu.SemaphoreType.DMA((45,)),
            pltpu.SemaphoreType.DMA((45,)),
        ],
        compiler_params=pltpu.CompilerParams(
            collective_id=0, has_side_effects=True, vmem_limit_bytes=60 * 1024 * 1024
        ),
        name="parareal",
    )(u, s, d, f, down, lat, heat, look)


def solution(mesh):
    return jax.shard_map(
        functools.partial(per_device, mesh.shape["tm"], mesh.shape["space"]),
        mesh=mesh,
        in_specs=(
            P(None, "space", None),
            P("space", None),
            P("space", None),
            P(None, "space", None),
            P(None, None, "space", None),
            P(None, None, "space", None),
            P(),
            P("tm"),
        ),
        out_specs=(P("tm", None, "space", None), P("tm", "space", None)),
        check_vma=False,
    )
```

```python
import functools

import jax
import jax.numpy as jnp
from jax import lax
from jax.experimental import pallas as pl
from jax.experimental.pallas import tpu as pltpu
from jax.sharding import PartitionSpec as P

COUPLING = 0.9 / 6.4
MASS = 0.3
HARDENING = 0.25
SATURATION = 3.0
TICK = 0.5
HALF_WIDTH = 0.9
SWEEPS = 8
ANAND = 4
ROWS = 26
OWN = 9
ABOVE, BELOW = 1, 17
PLANES = 26
S0, D0, U0, F0, L0 = 0, 9, 10, 14, 17
MESH = pl.DeviceIdType.MESH


def chebyshev_weights():
    weights, w = [], HALF_WIDTH
    for _ in range(SWEEPS - 1):
        nxt = 1.0 / (2.0 / HALF_WIDTH - w)
        weights.append((nxt * w, 2.0 * nxt / HALF_WIDTH))
        w = nxt
    return weights


def at(row):
    if isinstance(row, int):
        return pl.ds(8 * row, 8)
    return pl.ds(pl.multiple_of(8 * row, 8), 8)


def span(row, count):
    if isinstance(row, int):
        return pl.ds(8 * row, 8 * count)
    return pl.ds(pl.multiple_of(8 * row, 8), 8 * count)


def kernel(
    n_tm, n_sp,
    u_hbm, s_hbm, d_hbm, f_hbm, down_hbm, lat_hbm, heat_hbm, look_hbm,
    u_out, s_out,
    u_in, s_in, d_in, f_in, down_in, lat_in, heat, look,
    raw, DI, U, Pd, Z, E, GU, C, VOUT, VIN, CIN, XH, TH, lsem, ssem, rsem,
):
    n = lax.axis_index("tm")
    sp = lax.axis_index("space")
    up, dn = lax.rem(sp + n_sp - 1, n_sp), lax.rem(sp + 1, n_sp)
    up2, dn2 = lax.rem(sp + n_sp - 2, n_sp), lax.rem(sp + 2, n_sp)
    lane = lax.broadcasted_iota(jnp.int32, (8, 128), 1)
    sub = lax.broadcasted_iota(jnp.int32, (8, 128), 0)
    first_lane, last_lane = lane == 0, lane == 127

    loads = [
        pltpu.make_async_copy(src, dst, lsem.at[k])
        for k, (src, dst) in enumerate(
            [(look_hbm, look), (heat_hbm, heat), (down_hbm, down_in), (lat_hbm, lat_in),
             (u_hbm, u_in), (s_hbm, s_in), (d_hbm, d_in), (f_hbm, f_in)]
        )
    ]
    for c in loads:
        c.start()

    barrier = pltpu.get_barrier_semaphore()
    peers = [(lax.rem(n + d, n_tm), sp) for d in range(1, n_tm)]
    for d in (0, 1, 2, n_tm - 2, n_tm - 1):
        for side in (up, dn):
            peers.append((lax.rem(n + d, n_tm), side))
    peers += [(n, up2), (n, dn2)]
    for peer in peers:
        pl.semaphore_signal(barrier, inc=1, device_id=peer, device_id_type=MESH)

    def copy(src, dst, sem, who):
        return pltpu.make_async_remote_copy(
            src_ref=src, dst_ref=dst, send_sem=ssem.at[sem], recv_sem=rsem.at[sem],
            device_id=who, device_id_type=MESH,
        )

    def pack(plane, tile_of):
        for c in range(8):
            raw[plane, pl.ds(8 * OWN + c, 8, stride=8), :] = tile_of(pl.ds(128 * c, 128))

    for c in loads:
        c.wait()
    for a in range(3):
        for b in range(3):
            pack(S0 + 3 * a + b, lambda cols, a=a, b=b: down_in[a, b, :, cols])
            pack(L0 + 3 * a + b, lambda cols, a=a, b=b: lat_in[a, b, :, cols])
        pack(F0 + a, lambda cols, a=a: f_in[a, :, cols])
        pack(U0 + a, lambda cols, a=a: u_in[a, :, cols])
    pack(D0, lambda cols: d_in[:, cols])
    pack(U0 + 3, lambda cols: s_in[:, cols])
    for k in range(2):
        TH[n, pl.ds(8 * k, 8), :] = jnp.full((8, 128), heat[look[k]], jnp.float32)

    pl.semaphore_wait(barrier, len(peers))

    core = lax.rem(sp, 2)
    y = n // 2
    sibling = sp + 1 - 2 * core
    outer = jnp.where(core == 0, up, dn)
    to_sibling = jnp.where(core == 0, ABOVE, BELOW)
    to_outer = jnp.where(core == 0, BELOW, ABOVE)
    from_outer = jnp.where(core == 0, ABOVE, BELOW)
    across = (n + 1 - 2 * lax.rem(n, 2), outer)
    shared = copy(raw.at[:, span(OWN + y, 1), :], raw.at[:, span(to_outer + y, 1), :], 1, across)
    shared.start()
    straight = [
        copy(raw.at[:, span(OWN + 4, 4), :], raw.at[:, span(to_outer + 4, 4), :], 2, across),
        copy(raw.at[:, span(OWN, 8), :], raw.at[:, span(to_sibling, 8), :], 0, (n, sibling)),
        copy(
            raw.at[pl.ds(0, F0 - 1), span(OWN + 7, 1), :],
            raw.at[pl.ds(0, F0 - 1), span(0, 1), :], 6, (n, dn2),
        ),
        copy(
            raw.at[pl.ds(D0, 4), span(OWN, 1), :],
            raw.at[pl.ds(D0, 4), span(ROWS - 1, 1), :], 7, (n, up2),
        ),
    ]
    heats = [
        copy(TH.at[n], TH.at[n], 7 + d, (lax.rem(n + d, n_tm), sp)) for d in range(1, n_tm)
    ]
    for c in straight + heats:
        c.start()
    shared.wait_recv()
    passed = raw.at[:, span(from_outer + y, 1), :]
    passing = [
        copy(passed, passed, 2 + d, (lax.rem(n + 2 * d, n_tm), sp)) for d in (1, 2, 3)
    ]
    for c in passing:
        c.start()
    for d in range(1, n_tm):
        src = lax.rem(n + n_tm - d, n_tm)
        copy(TH.at[src], TH.at[src], 7 + d, (src, sp)).wait_recv()
    for c in straight:
        c.wait()
    for d in (1, 2, 3):
        src = lax.rem(n + n_tm - 2 * d, n_tm)
        row = raw.at[:, span(from_outer + src // 2, 1), :]
        copy(row, row, 2 + d, (src, sp)).wait_recv()
    shared.wait_send()
    for c in heats + passing:
        c.wait_send()

    def east(v):
        a = pltpu.roll(v, 127, 1)
        return jnp.where(last_lane, pltpu.roll(a, 7, 0), a)

    def west(v):
        a = pltpu.roll(v, 1, 1)
        return jnp.where(first_lane, pltpu.roll(a, 1, 0), a)

    corner = (lane == 127) & (sub == 7)
    for r in range(ROWS):
        diag = raw[D0, at(r), :]
        if r < ROWS - 1:
            row = 8 * sp + (r - OWN)
            seam = (row == -1) | (row == 8 * n_sp - 1)
            below = raw[D0, at(r + 1), :]
            cs = COUPLING * jnp.minimum(diag, below) * jnp.where(seam, 0.0, 1.0)
            for k in range(9):
                raw[S0 + k, at(r), :] = raw[S0 + k, at(r), :] * cs
        if 0 < r < ROWS - 1:
            cl = jnp.where(corner, 0.0, COUPLING * jnp.minimum(diag, east(diag)))
            for k in range(9):
                raw[L0 + k, at(r), :] = raw[L0 + k, at(r), :] * cl
            DI[at(r), :] = 1.0 / diag
            U[3, at(r), :] = raw[U0 + 3, at(r), :]
        for k in range(3):
            U[k, at(r), :] = raw[U0 + k, at(r), :]

    def heat_of(slice_index, tick):
        return TH[slice_index, pl.ds(8 * tick, 1), :]

    def mean_heat(slice_index):
        return 0.5 * (TH[slice_index, 0:1, :] + TH[slice_index, 8:9, :])

    def creep(load, store_s, t, h, lo, count, chunk):
        rate = jnp.exp(2.0 - 2.0 / t)

        def body(i, _):
            r = lo + i * chunk
            u0, u1, u2, s = (load(k, r, chunk) for k in range(4))
            q2 = (u0 * u0 + u1 * u1 + u2 * u2) * (1.0 / 3.0) + 1.0
            qi = lax.rsqrt(q2)
            q = q2 * qi
            x = s
            for _ in range(ANAND):
                x = s + (h * HARDENING) * rate * jnp.tanh(q / x) * (1.0 - x * (1.0 / SATURATION))
            E[span(r, chunk), :] = (h * rate) * jnp.tanh(q / x) * qi
            store_s(r, chunk, x)
            return 0

        lax.fori_loop(0, count // chunk, body, 0)

    def stencil(load, lo, hi, emit):
        p = [load(b, lo - 1) for b in range(3)]
        s = [[raw[S0 + 3 * a + b, at(lo - 1), :] for b in range(3)] for a in range(3)]
        north = [s[0][b] * p[0] + s[1][b] * p[1] + s[2][b] * p[2] for b in range(3)]
        p = [load(b, lo) for b in range(3)]
        for r in range(lo, hi):
            nxt = [load(b, r + 1) for b in range(3)]
            s = [[raw[S0 + 3 * a + b, at(r), :] for b in range(3)] for a in range(3)]
            l = [[raw[L0 + 3 * a + b, at(r), :] for b in range(3)] for a in range(3)]
            pe = [east(p[b]) for b in range(3)]
            wf = [west(l[0][b] * p[0] + l[1][b] * p[1] + l[2][b] * p[2]) for b in range(3)]
            cv = []
            for a in range(3):
                south = s[a][0] * nxt[0] + s[a][1] * nxt[1] + s[a][2] * nxt[2]
                right = l[a][0] * pe[0] + l[a][1] * pe[1] + l[a][2] * pe[2]
                cv.append((north[a] + wf[a]) + (south + right))
            north = [s[0][b] * p[0] + s[1][b] * p[1] + s[2][b] * p[2] for b in range(3)]
            emit(r, p, cv)
            p = nxt

    def force(r, v, cv, th):
        inv, e = DI[at(r), :], E[at(r), :]
        return [
            inv * (th * raw[F0 + a, at(r), :] - e * v[a] - cv[a]) for a in range(3)
        ]

    def fine_tick(t):
        h = TICK

        def load(k, r, c):
            return U[k, span(r, c), :]

        def store_s(r, c, x):
            U[3, span(r, c), :] = x

        creep(load, store_s, t, h, 1, ROWS - 2, 12)
        th = h * t

        def first(r, v, cv):
            g = force(r, v, cv, th)
            for a in range(3):
                z = g[a] - (1.0 - MASS) * v[a]
                Z[a, at(r), :] = z
                Pd[a, at(r), :] = z
                if OWN <= r < OWN + 8:
                    U[a, at(r), :] = v[a] + z

        stencil(lambda b, r: U[b, at(r), :], 2, ROWS - 2, first)
        for k, (alpha, beta) in enumerate(chebyshev_weights()):
            def sweep(r, v, cv, alpha=alpha, beta=beta, k=k):
                inv = DI[at(r), :]
                for a in range(3):
                    z = Z[a, at(r), :] - v[a] - inv * cv[a]
                    p = alpha * v[a] + beta * z
                    if k < SWEEPS - 2:
                        Z[a, at(r), :] = z
                        Pd[a, at(r), :] = p
                    if OWN <= r < OWN + 8:
                        U[a, at(r), :] = U[a, at(r), :] + p

            stencil(lambda b, r: Pd[b, at(r), :], 3 + k, ROWS - 3 - k, sweep)

    def exchange(slot, sem, planes, between=None):
        own = U.at[pl.ds(0, planes), span(OWN, 8), :]
        pair = [
            copy(own, XH.at[slot, 0, pl.ds(0, planes)], sem, (n, dn)),
            copy(own, XH.at[slot, 1, pl.ds(0, planes)], sem + 1, (n, up)),
        ]
        for c in pair:
            c.start()
        if between is not None:
            between()
        for c in pair:
            c.wait()
        for k in range(planes):
            U[k, span(ABOVE, 8), :] = XH[slot, 0, k]
            U[k, span(BELOW, 8), :] = XH[slot, 1, k]

    def coarse_own(src):
        t = mean_heat(n)

        def load(k, r, c):
            return src[k, span(r, c), :]

        def store_s(r, c, x):
            GU[3, span(r - OWN, c), :] = x

        creep(load, store_s, t, 2.0 * TICK, OWN, 8, 8)

        def emit(r, v, cv):
            g = force(r, v, cv, 2.0 * TICK * t)
            for a in range(3):
                GU[a, at(r - OWN), :] = MASS * v[a] + g[a]

        stencil(lambda b, r: src[b, at(r), :], OWN, OWN + 8, emit)

    def coarse_step(m, _):
        t = mean_heat(m)

        def load(k, r, c):
            return U[k, span(r, c), :]

        def store_s(r, c, x):
            U[3, span(r, c), :] = x

        creep(load, store_s, t, 2.0 * TICK, 1, ROWS - 2, 12)

        def emit(r, v, cv):
            g = force(r, v, cv, 2.0 * TICK * t)
            for a in range(3):
                U[a, at(r), :] = MASS * v[a] + g[a]

        stencil(lambda b, r: U[b, at(r), :], 1, ROWS - 1, emit)
        return 0

    lax.fori_loop(0, n, coarse_step, 0)

    @pl.when(n == 1)
    def _():
        coarse_own(U)

    @pl.when(n > 1)
    def _():
        exchange(0, 15, 4, lambda: coarse_own(U))

    odd = lax.rem(n, 2) == 1
    even = (lax.rem(n, 2) == 0) & (n > 0)
    hands_on = odd & (n < n_tm - 1)
    joins = odd & (n > 1)

    def trimmed(src, dst, rows, base, who):
        return [
            copy(src.at[:, span(0, rows), :], dst.at[:, span(BELOW, rows), :], base + 1, (who, up)),
            copy(
                src.at[:, span(8 - rows, rows), :], dst.at[:, span(OWN - rows, rows), :],
                base + 2, (who, dn),
            ),
            copy(src, dst.at[:, span(OWN, 8), :], base, (who, sp)),
        ]

    def whole_halo(base, who):
        return copy(VOUT.at[0], VIN.at[0, :, span(to_outer, 8), :], base, (who, outer))

    def beside(slot):
        own = VIN.at[slot, :, span(OWN, 8), :]
        return copy(own, VIN.at[0, :, span(to_sibling, 8), :], 25, (n, sibling))

    def to_first():
        return trimmed(VOUT.at[0], VIN.at[1], 1, 41, 1) + [whole_halo(44, 1)]

    def to_next(p):
        nxt = lax.rem(n + 1, n_tm)
        if p == 0:
            own = copy(VOUT.at[0], VIN.at[0, :, span(OWN, 8), :], 23, (nxt, sp))
            return [own, whole_halo(24, nxt)]
        return trimmed(VOUT.at[1], VIN.at[1], 1, 29, nxt)

    def to_second(p):
        return trimmed(VOUT.at[p], VIN.at[p], 2, 26 + 6 * p, lax.rem(n + 2, n_tm))

    def corrections(p):
        return trimmed(C.at[p], CIN.at[p], 1, 35 + 3 * p, lax.rem(n + 1, n_tm))

    def corrected(load, corr, dst, t, lo, count):
        def store_s(r, c, x):
            dst[3, span(r, c), :] = x * corr[3, span(r, c), :]

        creep(load, store_s, t, 2.0 * TICK, lo, count, count)

        def emit(r, v, cv):
            g = force(r, v, cv, 2.0 * TICK * t)
            for a in range(3):
                dst[a, at(r), :] = MASS * v[a] + g[a] + corr[a, at(r), :]

        stencil(lambda b, r: load(b, r, 1), lo, lo + count, emit)

    def one_pass(p, _):
        @pl.when((n > 0) | (p == 0))
        def _():
            def tick(i, _):
                @pl.when(i == 1)
                def _():
                    def meanwhile():
                        @pl.when(even & (p == 1))
                        def _():
                            coarse_own(VIN.at[0])

                    exchange(1 + 2 * p, 17 + 4 * p, 3, meanwhile)

                fine_tick(heat_of(n, i))
                return 0

            lax.fori_loop(0, 2, tick, 0)

        @pl.when(n > 0)
        def _():
            for a in range(3):
                C[p, a] = U[a, span(OWN, 8), :] - GU[a]
            C[p, 3] = U[3, span(OWN, 8), :] / GU[3]

        @pl.when(even)
        def _():
            for c in corrections(p):
                c.start()

        @pl.when((n == 1) & (p == 0))
        def _():
            for c in to_first()[:3]:
                c.wait_recv()

        @pl.when(even & (p == 0))
        def _():
            own, halo = to_next(0)
            own.wait_recv()
            pair = beside(0)
            pair.start()
            pair.wait()
            halo.wait_recv()
            for k in range(4):
                for r in (ABOVE, OWN, BELOW):
                    U[k, span(r, 8), :] = VIN[0, k, span(r, 8), :]

        @pl.when(even & (p == 1))
        def _():
            for c in to_next(1):
                c.wait_recv()

        @pl.when((n == 1) | (even & (p == 1)))
        def _():
            for k in range(4):
                U[k, span(OWN - 1, 10), :] = VIN[1, k, span(OWN - 1, 10), :]

        @pl.when(joins)
        def _():
            for c in corrections(p):
                c.wait_recv()
            for c in to_second(p):
                c.wait_recv()
            corrected(
                lambda k, r, c: VIN[p, k, span(r, c), :], CIN.at[p], U,
                mean_heat(n - 1), OWN - 1, 10,
            )

        @pl.when(n == 0)
        def _():
            for k in range(4):
                VOUT[p, k] = U[k, span(OWN, 8), :]

        def pass_on():
            @pl.when((n > 0) & jnp.logical_not(even & (p == 0)))
            def _():
                coarse_own(U)
                for a in range(3):
                    VOUT[p, a] = GU[a] + C[p, a]
                VOUT[p, 3] = GU[3] * C[p, 3]

            @pl.when((n == 0) & (p == 0))
            def _():
                for c in to_first():
                    c.start()

            next_first = (n == n_tm - 3) & (p == 0)

            @pl.when(next_first)
            def _():
                for c in to_next(0):
                    c.start()

            @pl.when(hands_on)
            def _():
                for c in to_second(p):
                    c.start()

            @pl.when(hands_on & (n < n_tm - 3) & (p == 0))
            def _():
                for c in to_next(0):
                    c.start()

            @pl.when(hands_on & (p == 1))
            def _():
                for c in to_next(1):
                    c.start()

        halo_now = joins & (p == 0)

        @pl.when(halo_now)
        def _():
            exchange(2, 19, 4, pass_on)

        @pl.when(jnp.logical_not(halo_now))
        def _():
            pass_on()

        @pl.when((n == 1) & (p == 0))
        def _():
            pair = beside(1)
            pair.start()
            pair.wait()
            to_first()[3].wait_recv()
            for k in range(4):
                for r in (ABOVE, BELOW):
                    U[k, span(r, 8), :] = VIN[0, k, span(r, 8), :]

        return 0

    lax.fori_loop(0, 2, one_pass, 0)

    for c in range(8):
        cols = pl.ds(128 * c, 128)
        for a in range(3):
            u_out[0, a, :, cols] = VOUT[1, a, pl.ds(c, 8, stride=8), :]
        s_out[0, :, cols] = VOUT[1, 3, pl.ds(c, 8, stride=8), :]

    @pl.when(n == 0)
    def _():
        for c in to_first():
            c.wait_send()

    for p in range(2):
        @pl.when(even)
        def _():
            for c in corrections(p):
                c.wait_send()

        @pl.when(hands_on)
        def _():
            for c in to_next(p) + to_second(p):
                c.wait_send()


def per_device(n_tm, n_sp, u, s, d, f, down, lat, heat, look):
    vmem = pl.BlockSpec(memory_space=pltpu.VMEM)
    hbm = pl.BlockSpec(memory_space=pl.ANY)
    f32 = jnp.float32
    inputs = (u, s, d, f, down, lat)
    return pl.pallas_call(
        functools.partial(kernel, n_tm, n_sp),
        out_shape=(
            jax.ShapeDtypeStruct((1, 3, 8, 1024), f32),
            jax.ShapeDtypeStruct((1, 8, 1024), f32),
        ),
        in_specs=[hbm] * 8,
        out_specs=(vmem, vmem),
        scratch_shapes=[pltpu.VMEM(x.shape, f32) for x in inputs] + [
            pltpu.SMEM(heat.shape, f32),
            pltpu.SMEM(look.shape, jnp.int32),
            pltpu.VMEM((PLANES, 8 * ROWS, 128), f32),
            pltpu.VMEM((8 * ROWS, 128), f32),
            pltpu.VMEM((4, 8 * ROWS, 128), f32),
            pltpu.VMEM((3, 8 * ROWS, 128), f32),
            pltpu.VMEM((3, 8 * ROWS, 128), f32),
            pltpu.VMEM((8 * ROWS, 128), f32),
            pltpu.VMEM((4, 64, 128), f32),
            pltpu.VMEM((2, 4, 64, 128), f32),
            pltpu.VMEM((2, 4, 64, 128), f32),
            pltpu.VMEM((2, 4, 8 * ROWS, 128), f32),
            pltpu.VMEM((2, 4, 8 * ROWS, 128), f32),
            pltpu.VMEM((4, 2, 4, 64, 128), f32),
            pltpu.VMEM((8, 16, 128), f32),
            pltpu.SemaphoreType.DMA((8,)),
            pltpu.SemaphoreType.DMA((45,)),
            pltpu.SemaphoreType.DMA((45,)),
        ],
        compiler_params=pltpu.CompilerParams(
            collective_id=0, has_side_effects=True, vmem_limit_bytes=60 * 1024 * 1024
        ),
        name="parareal",
    )(u, s, d, f, down, lat, heat, look)


def solution(mesh):
    return jax.shard_map(
        functools.partial(per_device, mesh.shape["tm"], mesh.shape["space"]),
        mesh=mesh,
        in_specs=(
            P(None, "space", None),
            P("space", None),
            P("space", None),
            P(None, "space", None),
            P(None, None, "space", None),
            P(None, None, "space", None),
            P(),
            P("tm"),
        ),
        out_specs=(P("tm", None, "space", None), P("tm", "space", None)),
        check_vma=False,
    )
```

```python
import functools

import jax
import jax.numpy as jnp
from jax import lax
from jax.experimental import pallas as pl
from jax.experimental.pallas import tpu as pltpu
from jax.sharding import PartitionSpec as P

COUPLING = 0.9 / 6.4
MASS = 0.3
HARDENING = 0.25
SATURATION = 3.0
TICK = 0.5
HALF_WIDTH = 0.9
SWEEPS = 8
ANAND = 4
ROWS = 26
OWN = 9
ABOVE, BELOW = 1, 17
PLANES = 26
S0, D0, U0, F0, L0 = 0, 9, 10, 14, 17
MESH = pl.DeviceIdType.MESH


def chebyshev_weights():
    weights, w = [], HALF_WIDTH
    for _ in range(SWEEPS - 1):
        nxt = 1.0 / (2.0 / HALF_WIDTH - w)
        weights.append((nxt * w, 2.0 * nxt / HALF_WIDTH))
        w = nxt
    return weights


def at(row):
    if isinstance(row, int):
        return pl.ds(8 * row, 8)
    return pl.ds(pl.multiple_of(8 * row, 8), 8)


def span(row, count):
    if isinstance(row, int):
        return pl.ds(8 * row, 8 * count)
    return pl.ds(pl.multiple_of(8 * row, 8), 8 * count)


def kernel(
    n_tm, n_sp,
    u_hbm, s_hbm, d_hbm, f_hbm, down_hbm, lat_hbm, heat_hbm, look_hbm,
    u_out, s_out,
    u_in, s_in, d_in, f_in, down_in, lat_in, heat, look,
    raw, DI, U, Pd, Z, E, GU, C, VOUT, VIN, CIN, XH, TH, lsem, ssem, rsem,
):
    n = lax.axis_index("tm")
    sp = lax.axis_index("space")
    up, dn = lax.rem(sp + n_sp - 1, n_sp), lax.rem(sp + 1, n_sp)
    up2, dn2 = lax.rem(sp + n_sp - 2, n_sp), lax.rem(sp + 2, n_sp)
    lane = lax.broadcasted_iota(jnp.int32, (8, 128), 1)
    sub = lax.broadcasted_iota(jnp.int32, (8, 128), 0)
    first_lane, last_lane = lane == 0, lane == 127

    loads = [
        pltpu.make_async_copy(src, dst, lsem.at[k])
        for k, (src, dst) in enumerate(
            [(look_hbm, look), (heat_hbm, heat), (down_hbm, down_in), (lat_hbm, lat_in),
             (u_hbm, u_in), (s_hbm, s_in), (d_hbm, d_in), (f_hbm, f_in)]
        )
    ]
    barrier = pltpu.get_barrier_semaphore()
    peers = [(lax.rem(n + d, n_tm), sp) for d in range(1, n_tm)]
    for d in (0, 1, 2, n_tm - 2, n_tm - 1):
        for side in (up, dn):
            peers.append((lax.rem(n + d, n_tm), side))
    peers += [(n, up2), (n, dn2)]
    for peer in peers:
        pl.semaphore_signal(barrier, inc=1, device_id=peer, device_id_type=MESH)

    for c in loads:
        c.start()

    def copy(src, dst, sem, who):
        return pltpu.make_async_remote_copy(
            src_ref=src, dst_ref=dst, send_sem=ssem.at[sem], recv_sem=rsem.at[sem],
            device_id=who, device_id_type=MESH,
        )

    def pack(plane, tile_of):
        for c in range(8):
            raw[plane, pl.ds(8 * OWN + c, 8, stride=8), :] = tile_of(pl.ds(128 * c, 128))

    for c in loads:
        c.wait()
    for a in range(3):
        for b in range(3):
            pack(S0 + 3 * a + b, lambda cols, a=a, b=b: down_in[a, b, :, cols])
            pack(L0 + 3 * a + b, lambda cols, a=a, b=b: lat_in[a, b, :, cols])
        pack(F0 + a, lambda cols, a=a: f_in[a, :, cols])
        pack(U0 + a, lambda cols, a=a: u_in[a, :, cols])
    pack(D0, lambda cols: d_in[:, cols])
    pack(U0 + 3, lambda cols: s_in[:, cols])
    for k in range(2):
        TH[n, pl.ds(8 * k, 8), :] = jnp.full((8, 128), heat[look[k]], jnp.float32)

    pl.semaphore_wait(barrier, len(peers))

    core = lax.rem(sp, 2)
    y = n // 2
    sibling = sp + 1 - 2 * core
    outer = jnp.where(core == 0, up, dn)
    to_sibling = jnp.where(core == 0, ABOVE, BELOW)
    to_outer = jnp.where(core == 0, BELOW, ABOVE)
    from_outer = jnp.where(core == 0, ABOVE, BELOW)
    across = (n + 1 - 2 * lax.rem(n, 2), outer)
    shared = copy(raw.at[:, span(OWN + y, 1), :], raw.at[:, span(to_outer + y, 1), :], 1, across)
    shared.start()
    straight = [
        copy(raw.at[:, span(OWN + 4, 4), :], raw.at[:, span(to_outer + 4, 4), :], 2, across),
        copy(raw.at[:, span(OWN, 8), :], raw.at[:, span(to_sibling, 8), :], 0, (n, sibling)),
        copy(
            raw.at[pl.ds(0, F0 - 1), span(OWN + 7, 1), :],
            raw.at[pl.ds(0, F0 - 1), span(0, 1), :], 6, (n, dn2),
        ),
        copy(
            raw.at[pl.ds(D0, 4), span(OWN, 1), :],
            raw.at[pl.ds(D0, 4), span(ROWS - 1, 1), :], 7, (n, up2),
        ),
    ]
    heats = [
        copy(TH.at[n], TH.at[n], 7 + d, (lax.rem(n + d, n_tm), sp)) for d in range(1, n_tm)
    ]
    for c in straight + heats:
        c.start()
    shared.wait_recv()
    passed = raw.at[:, span(from_outer + y, 1), :]
    passing = [
        copy(passed, passed, 2 + d, (lax.rem(n + 2 * d, n_tm), sp)) for d in (1, 2, 3)
    ]
    for c in passing:
        c.start()
    for d in range(1, n_tm):
        src = lax.rem(n + n_tm - d, n_tm)
        copy(TH.at[src], TH.at[src], 7 + d, (src, sp)).wait_recv()
    for c in straight:
        c.wait()
    for d in (1, 2, 3):
        src = lax.rem(n + n_tm - 2 * d, n_tm)
        row = raw.at[:, span(from_outer + src // 2, 1), :]
        copy(row, row, 2 + d, (src, sp)).wait_recv()
    shared.wait_send()
    for c in heats + passing:
        c.wait_send()

    def east(v):
        a = pltpu.roll(v, 127, 1)
        return jnp.where(last_lane, pltpu.roll(a, 7, 0), a)

    def west(v):
        a = pltpu.roll(v, 1, 1)
        return jnp.where(first_lane, pltpu.roll(a, 1, 0), a)

    corner = (lane == 127) & (sub == 7)
    for r in range(ROWS):
        diag = raw[D0, at(r), :]
        if r < ROWS - 1:
            row = 8 * sp + (r - OWN)
            seam = (row == -1) | (row == 8 * n_sp - 1)
            below = raw[D0, at(r + 1), :]
            cs = COUPLING * jnp.minimum(diag, below) * jnp.where(seam, 0.0, 1.0)
            for k in range(9):
                raw[S0 + k, at(r), :] = raw[S0 + k, at(r), :] * cs
        if 0 < r < ROWS - 1:
            cl = jnp.where(corner, 0.0, COUPLING * jnp.minimum(diag, east(diag)))
            for k in range(9):
                raw[L0 + k, at(r), :] = raw[L0 + k, at(r), :] * cl
            DI[at(r), :] = 1.0 / diag
            U[3, at(r), :] = raw[U0 + 3, at(r), :]
        for k in range(3):
            U[k, at(r), :] = raw[U0 + k, at(r), :]

    def heat_of(slice_index, tick):
        return TH[slice_index, pl.ds(8 * tick, 1), :]

    def mean_heat(slice_index):
        return 0.5 * (TH[slice_index, 0:1, :] + TH[slice_index, 8:9, :])

    def creep(load, store_s, t, h, lo, count, chunk):
        rate = jnp.exp(2.0 - 2.0 / t)

        def body(i, _):
            r = lo + i * chunk
            u0, u1, u2, s = (load(k, r, chunk) for k in range(4))
            q2 = (u0 * u0 + u1 * u1 + u2 * u2) * (1.0 / 3.0) + 1.0
            qi = lax.rsqrt(q2)
            q = q2 * qi
            x = s
            for _ in range(ANAND):
                x = s + (h * HARDENING) * rate * jnp.tanh(q / x) * (1.0 - x * (1.0 / SATURATION))
            E[span(r, chunk), :] = (h * rate) * jnp.tanh(q / x) * qi
            store_s(r, chunk, x)
            return 0

        lax.fori_loop(0, count // chunk, body, 0)

    def stencil(load, lo, hi, emit):
        p = [load(b, lo - 1) for b in range(3)]
        s = [[raw[S0 + 3 * a + b, at(lo - 1), :] for b in range(3)] for a in range(3)]
        north = [s[0][b] * p[0] + s[1][b] * p[1] + s[2][b] * p[2] for b in range(3)]
        p = [load(b, lo) for b in range(3)]
        for r in range(lo, hi):
            nxt = [load(b, r + 1) for b in range(3)]
            s = [[raw[S0 + 3 * a + b, at(r), :] for b in range(3)] for a in range(3)]
            l = [[raw[L0 + 3 * a + b, at(r), :] for b in range(3)] for a in range(3)]
            pe = [east(p[b]) for b in range(3)]
            wf = [west(l[0][b] * p[0] + l[1][b] * p[1] + l[2][b] * p[2]) for b in range(3)]
            cv = []
            for a in range(3):
                south = s[a][0] * nxt[0] + s[a][1] * nxt[1] + s[a][2] * nxt[2]
                right = l[a][0] * pe[0] + l[a][1] * pe[1] + l[a][2] * pe[2]
                cv.append((north[a] + wf[a]) + (south + right))
            north = [s[0][b] * p[0] + s[1][b] * p[1] + s[2][b] * p[2] for b in range(3)]
            emit(r, p, cv)
            p = nxt

    def force(r, v, cv, th):
        inv, e = DI[at(r), :], E[at(r), :]
        return [
            inv * (th * raw[F0 + a, at(r), :] - e * v[a] - cv[a]) for a in range(3)
        ]

    def fine_tick(t):
        h = TICK

        def load(k, r, c):
            return U[k, span(r, c), :]

        def store_s(r, c, x):
            U[3, span(r, c), :] = x

        creep(load, store_s, t, h, 1, ROWS - 2, 12)
        th = h * t

        def first(r, v, cv):
            g = force(r, v, cv, th)
            for a in range(3):
                z = g[a] - (1.0 - MASS) * v[a]
                Z[a, at(r), :] = z
                Pd[a, at(r), :] = z
                if OWN <= r < OWN + 8:
                    U[a, at(r), :] = v[a] + z

        stencil(lambda b, r: U[b, at(r), :], 2, ROWS - 2, first)
        for k, (alpha, beta) in enumerate(chebyshev_weights()):
            def sweep(r, v, cv, alpha=alpha, beta=beta, k=k):
                inv = DI[at(r), :]
                for a in range(3):
                    z = Z[a, at(r), :] - v[a] - inv * cv[a]
                    p = alpha * v[a] + beta * z
                    if k < SWEEPS - 2:
                        Z[a, at(r), :] = z
                        Pd[a, at(r), :] = p
                    if OWN <= r < OWN + 8:
                        U[a, at(r), :] = U[a, at(r), :] + p

            stencil(lambda b, r: Pd[b, at(r), :], 3 + k, ROWS - 3 - k, sweep)

    def exchange(slot, sem, planes, between=None):
        own = U.at[pl.ds(0, planes), span(OWN, 8), :]
        pair = [
            copy(own, XH.at[slot, 0, pl.ds(0, planes)], sem, (n, dn)),
            copy(own, XH.at[slot, 1, pl.ds(0, planes)], sem + 1, (n, up)),
        ]
        for c in pair:
            c.start()
        if between is not None:
            between()
        for c in pair:
            c.wait()
        for k in range(planes):
            U[k, span(ABOVE, 8), :] = XH[slot, 0, k]
            U[k, span(BELOW, 8), :] = XH[slot, 1, k]

    def coarse_own(src):
        t = mean_heat(n)

        def load(k, r, c):
            return src[k, span(r, c), :]

        def store_s(r, c, x):
            GU[3, span(r - OWN, c), :] = x

        creep(load, store_s, t, 2.0 * TICK, OWN, 8, 8)

        def emit(r, v, cv):
            g = force(r, v, cv, 2.0 * TICK * t)
            for a in range(3):
                GU[a, at(r - OWN), :] = MASS * v[a] + g[a]

        stencil(lambda b, r: src[b, at(r), :], OWN, OWN + 8, emit)

    def coarse_step(m, _):
        t = mean_heat(m)

        def load(k, r, c):
            return U[k, span(r, c), :]

        def store_s(r, c, x):
            U[3, span(r, c), :] = x

        creep(load, store_s, t, 2.0 * TICK, 1, ROWS - 2, 12)

        def emit(r, v, cv):
            g = force(r, v, cv, 2.0 * TICK * t)
            for a in range(3):
                U[a, at(r), :] = MASS * v[a] + g[a]

        stencil(lambda b, r: U[b, at(r), :], 1, ROWS - 1, emit)
        return 0

    lax.fori_loop(0, n, coarse_step, 0)

    @pl.when(n == 1)
    def _():
        coarse_own(U)

    @pl.when(n > 1)
    def _():
        exchange(0, 15, 4, lambda: coarse_own(U))

    odd = lax.rem(n, 2) == 1
    even = (lax.rem(n, 2) == 0) & (n > 0)
    hands_on = odd & (n < n_tm - 1)
    joins = odd & (n > 1)

    def trimmed(src, dst, rows, base, who):
        return [
            copy(src.at[:, span(0, rows), :], dst.at[:, span(BELOW, rows), :], base + 1, (who, up)),
            copy(
                src.at[:, span(8 - rows, rows), :], dst.at[:, span(OWN - rows, rows), :],
                base + 2, (who, dn),
            ),
            copy(src, dst.at[:, span(OWN, 8), :], base, (who, sp)),
        ]

    def whole_halo(base, who):
        return copy(VOUT.at[0], VIN.at[0, :, span(to_outer, 8), :], base, (who, outer))

    def beside(slot):
        own = VIN.at[slot, :, span(OWN, 8), :]
        return copy(own, VIN.at[0, :, span(to_sibling, 8), :], 25, (n, sibling))

    def to_first():
        return trimmed(VOUT.at[0], VIN.at[1], 1, 41, 1) + [whole_halo(44, 1)]

    def to_next(p):
        nxt = lax.rem(n + 1, n_tm)
        if p == 0:
            own = copy(VOUT.at[0], VIN.at[0, :, span(OWN, 8), :], 23, (nxt, sp))
            return [own, whole_halo(24, nxt)]
        return trimmed(VOUT.at[1], VIN.at[1], 1, 29, nxt)

    def to_second(p):
        return trimmed(VOUT.at[p], VIN.at[p], 2, 26 + 6 * p, lax.rem(n + 2, n_tm))

    def corrections(p):
        return trimmed(C.at[p], CIN.at[p], 1, 35 + 3 * p, lax.rem(n + 1, n_tm))

    def corrected(load, corr, dst, t, lo, count):
        def store_s(r, c, x):
            dst[3, span(r, c), :] = x * corr[3, span(r, c), :]

        creep(load, store_s, t, 2.0 * TICK, lo, count, count)

        def emit(r, v, cv):
            g = force(r, v, cv, 2.0 * TICK * t)
            for a in range(3):
                dst[a, at(r), :] = MASS * v[a] + g[a] + corr[a, at(r), :]

        stencil(lambda b, r: load(b, r, 1), lo, lo + count, emit)

    def one_pass(p, _):
        @pl.when((n > 0) | (p == 0))
        def _():
            def tick(i, _):
                @pl.when(i == 1)
                def _():
                    def meanwhile():
                        @pl.when(even & (p == 1))
                        def _():
                            coarse_own(VIN.at[0])

                    exchange(1 + 2 * p, 17 + 4 * p, 3, meanwhile)

                fine_tick(heat_of(n, i))
                return 0

            lax.fori_loop(0, 2, tick, 0)

        @pl.when(n > 0)
        def _():
            for a in range(3):
                C[p, a] = U[a, span(OWN, 8), :] - GU[a]
            C[p, 3] = U[3, span(OWN, 8), :] / GU[3]

        @pl.when(even)
        def _():
            for c in corrections(p):
                c.start()

        @pl.when((n == 1) & (p == 0))
        def _():
            for c in to_first()[:3]:
                c.wait_recv()

        @pl.when(even & (p == 0))
        def _():
            own, halo = to_next(0)
            own.wait_recv()
            pair = beside(0)
            pair.start()
            pair.wait()
            halo.wait_recv()
            for k in range(4):
                for r in (ABOVE, OWN, BELOW):
                    U[k, span(r, 8), :] = VIN[0, k, span(r, 8), :]

        @pl.when(even & (p == 1))
        def _():
            for c in to_next(1):
                c.wait_recv()

        @pl.when((n == 1) | (even & (p == 1)))
        def _():
            for k in range(4):
                U[k, span(OWN - 1, 10), :] = VIN[1, k, span(OWN - 1, 10), :]

        @pl.when(joins)
        def _():
            for c in corrections(p):
                c.wait_recv()
            for c in to_second(p):
                c.wait_recv()
            corrected(
                lambda k, r, c: VIN[p, k, span(r, c), :], CIN.at[p], U,
                mean_heat(n - 1), OWN - 1, 10,
            )

        @pl.when(n == 0)
        def _():
            for k in range(4):
                VOUT[p, k] = U[k, span(OWN, 8), :]

        def pass_on():
            @pl.when((n > 0) & jnp.logical_not(even & (p == 0)))
            def _():
                coarse_own(U)
                for a in range(3):
                    VOUT[p, a] = GU[a] + C[p, a]
                VOUT[p, 3] = GU[3] * C[p, 3]

            @pl.when((n == 0) & (p == 0))
            def _():
                for c in to_first():
                    c.start()

            next_first = (n == n_tm - 3) & (p == 0)

            @pl.when(next_first)
            def _():
                for c in to_next(0):
                    c.start()

            @pl.when(hands_on)
            def _():
                for c in to_second(p):
                    c.start()

            @pl.when(hands_on & (n < n_tm - 3) & (p == 0))
            def _():
                for c in to_next(0):
                    c.start()

            @pl.when(hands_on & (p == 1))
            def _():
                for c in to_next(1):
                    c.start()

        halo_now = joins & (p == 0)

        @pl.when(halo_now)
        def _():
            exchange(2, 19, 4, pass_on)

        @pl.when(jnp.logical_not(halo_now))
        def _():
            pass_on()

        @pl.when((n == 1) & (p == 0))
        def _():
            pair = beside(1)
            pair.start()
            pair.wait()
            to_first()[3].wait_recv()
            for k in range(4):
                for r in (ABOVE, BELOW):
                    U[k, span(r, 8), :] = VIN[0, k, span(r, 8), :]

        return 0

    lax.fori_loop(0, 2, one_pass, 0)

    for c in range(8):
        cols = pl.ds(128 * c, 128)
        for a in range(3):
            u_out[0, a, :, cols] = VOUT[1, a, pl.ds(c, 8, stride=8), :]
        s_out[0, :, cols] = VOUT[1, 3, pl.ds(c, 8, stride=8), :]

    @pl.when(n == 0)
    def _():
        for c in to_first():
            c.wait_send()

    for p in range(2):
        @pl.when(even)
        def _():
            for c in corrections(p):
                c.wait_send()

        @pl.when(hands_on)
        def _():
            for c in to_next(p) + to_second(p):
                c.wait_send()


def per_device(n_tm, n_sp, u, s, d, f, down, lat, heat, look):
    vmem = pl.BlockSpec(memory_space=pltpu.VMEM)
    hbm = pl.BlockSpec(memory_space=pl.ANY)
    f32 = jnp.float32
    inputs = (u, s, d, f, down, lat)
    return pl.pallas_call(
        functools.partial(kernel, n_tm, n_sp),
        out_shape=(
            jax.ShapeDtypeStruct((1, 3, 8, 1024), f32),
            jax.ShapeDtypeStruct((1, 8, 1024), f32),
        ),
        in_specs=[hbm] * 8,
        out_specs=(vmem, vmem),
        scratch_shapes=[pltpu.VMEM(x.shape, f32) for x in inputs] + [
            pltpu.SMEM(heat.shape, f32),
            pltpu.SMEM(look.shape, jnp.int32),
            pltpu.VMEM((PLANES, 8 * ROWS, 128), f32),
            pltpu.VMEM((8 * ROWS, 128), f32),
            pltpu.VMEM((4, 8 * ROWS, 128), f32),
            pltpu.VMEM((3, 8 * ROWS, 128), f32),
            pltpu.VMEM((3, 8 * ROWS, 128), f32),
            pltpu.VMEM((8 * ROWS, 128), f32),
            pltpu.VMEM((4, 64, 128), f32),
            pltpu.VMEM((2, 4, 64, 128), f32),
            pltpu.VMEM((2, 4, 64, 128), f32),
            pltpu.VMEM((2, 4, 8 * ROWS, 128), f32),
            pltpu.VMEM((2, 4, 8 * ROWS, 128), f32),
            pltpu.VMEM((4, 2, 4, 64, 128), f32),
            pltpu.VMEM((8, 16, 128), f32),
            pltpu.SemaphoreType.DMA((8,)),
            pltpu.SemaphoreType.DMA((45,)),
            pltpu.SemaphoreType.DMA((45,)),
        ],
        compiler_params=pltpu.CompilerParams(
            collective_id=0, has_side_effects=True, vmem_limit_bytes=60 * 1024 * 1024
        ),
        name="parareal",
    )(u, s, d, f, down, lat, heat, look)


def solution(mesh):
    return jax.shard_map(
        functools.partial(per_device, mesh.shape["tm"], mesh.shape["space"]),
        mesh=mesh,
        in_specs=(
            P(None, "space", None),
            P("space", None),
            P("space", None),
            P(None, "space", None),
            P(None, None, "space", None),
            P(None, None, "space", None),
            P(),
            P("tm"),
        ),
        out_specs=(P("tm", None, "space", None), P("tm", "space", None)),
        check_vma=False,
    )
```
